32 devices in a mesh: seq: 4 (over x, core), ctx: 8 (over z, y).
Axes of the slice: x: 2, y: 2, z: 4, core: 2. Of those that a mesh axis runs over, the one named last changes fastest.
Arguments:
- hidden_in: bfloat16 [4, 1024, 2048], P('seq', 'ctx'), may hold values from -6 to 6
- positions: int32 [4, 1024], P('seq', 'ctx'), may hold values from 0 to 1023, as said below
- attn_gain: bfloat16 [2048], P(('seq', 'ctx')), may hold values from 0.25 to 1.75
- w_query: bfloat16 [2048, 2048], P(('seq', 'ctx')), may hold values from -0.125 to 0.125
- w_key: bfloat16 [2048, 2048], P(('seq', 'ctx')), may hold values from -0.125 to 0.125
- w_value: bfloat16 [2048, 2048], P(('seq', 'ctx')), may hold values from -0.125 to 0.125
- w_out: bfloat16 [2048, 2048], P(('seq', 'ctx')), may hold values from -0.75 to 0.75
- mlp_gain: bfloat16 [2048], P(('seq', 'ctx')), may hold values from 0.25 to 1.75
- w_gate: bfloat16 [2048, 8192], P(('seq', 'ctx')), may hold values from -0.125 to 0.125
- w_up: bfloat16 [2048, 8192], P(('seq', 'ctx')), may hold values from -0.125 to 0.125
- w_down: bfloat16 [8192, 2048], P(('seq', 'ctx')), may hold values from -0.0625 to 0.0625
- out_grad: bfloat16 [4, 1024, 2048], P('seq', 'ctx'), may hold values from -6 to 6
Outputs:
- hidden_out: bfloat16 [4, 1024, 2048], P('seq', 'ctx')
- hidden_grad: float32 [4, 1024, 2048], P('seq', 'ctx')
- attn_gain_grad: float32 [2048], P(('seq', 'ctx'))
- w_query_grad: float32 [2048, 2048], P(('seq', 'ctx'))
- w_key_grad: float32 [2048, 2048], P(('seq', 'ctx'))
- w_value_grad: float32 [2048, 2048], P(('seq', 'ctx'))
- w_out_grad: float32 [2048, 2048], P(('seq', 'ctx'))
- mlp_gain_grad: float32 [2048], P(('seq', 'ctx'))
- w_gate_grad: float32 [2048, 8192], P(('seq', 'ctx'))
- w_up_grad: float32 [2048, 8192], P(('seq', 'ctx'))
- w_down_grad: float32 [8192, 2048], P(('seq', 'ctx'))
The draws below stay inside these ranges and needn't reach their ends.
Inputs may be any that keep to these rules, and one draw needn't show every extreme that they name: In each sequence the positions are a permutation of 0 to 1023 made of 16 runs of 64 stored tokens, each run holding consecutive positions in increasing order; the order of the runs is drawn from the seed.
All inputs are finite; a program needn't handle non-finite values.
Results may differ from the reference program's by a relative error of at most 0.02.
Values may be sent and summed in bfloat16 or wider, within the bound.
No kernel may reach another device: no remote copies, remote signals or barrier semaphores. Data moves between devices by JAX's collectives and lax.ppermute only.
A program may use at most 704 MiB of HBM per device.

```python
import math
import jax
import jax.numpy as jnp
from jax import lax

D = 2048
HEADS = 32
HEAD_DIM = 64
FF = 8192
BLOCK = 64
LENGTH = 1024
SEQS = 4


def draw_positions(key, part):
    key = jax.random.fold_in(key, 11)
    sequence_keys = jax.random.split(key, SEQS)

    def one_sequence(seq_key):
        group_order = jax.random.permutation(seq_key, LENGTH // BLOCK).astype(jnp.int32)
        offsets = jnp.arange(BLOCK, dtype=jnp.int32)
        return (group_order[:, None] * BLOCK + offsets[None, :]).reshape(LENGTH)
    return jax.vmap(one_sequence)(sequence_keys).astype(jnp.int32)


def shard_levels(key, shape, cuts, low, largest):
    def one(axis_at, blocks):
        steps = jax.random.uniform(jax.random.fold_in(jax.random.fold_in(key, 6), axis_at), (blocks,), jnp.float32, low / len(cuts), largest / len(cuts))
        return jnp.repeat(jnp.exp(steps), shape[axis_at] // blocks).reshape((-1,) + (1,) * (len(shape) - axis_at - 1))

    gain = one(*cuts[0])
    for cut in cuts[1:]:
        gain = gain * one(*cut)
    return gain


def scatter_about(key, dims, width, bound, cuts=(), kind=jnp.bfloat16):
    array = width * jax.random.normal(key, dims, jnp.float32)
    if cuts:
        array = array * shard_levels(key, dims, cuts, -0.22, 0.18)
    return jnp.clip(array, -bound, bound).astype(kind)


def setup_inputs(seed: int = 0) -> dict:
    key_of = jax.random.split(jax.random.key(seed), 13)
    return {
        "hidden_in": scatter_about(key_of[0], (SEQS, LENGTH, D), 1.0, 6.0, ((0, 4), (1, 8))),
        "positions": draw_positions(jax.random.fold_in(key_of[12], 71), 0),
        "attn_gain": jnp.clip(1.0 + 0.15 * jax.random.normal(key_of[2], (D,), jnp.float32), 0.25, 1.75).astype(jnp.bfloat16),
        "w_query": scatter_about(key_of[3], (D, D), D ** -0.5, 0.125, ((0, 32),)),
        "w_key": scatter_about(key_of[4], (D, D), D ** -0.5, 0.125, ((0, 32),)),
        "w_value": scatter_about(key_of[5], (D, D), D ** -0.5, 0.125, ((0, 32),)),
        "w_out": scatter_about(key_of[6], (D, D), (D // 32) ** -0.5, 0.75, ((0, 32),)),
        "mlp_gain": jnp.clip(1.0 + 0.15 * jax.random.normal(key_of[7], (D,), jnp.float32), 0.25, 1.75).astype(jnp.bfloat16),
        "w_gate": scatter_about(key_of[8], (D, FF), D ** -0.5, 0.125, ((0, 32),)),
        "w_up": scatter_about(key_of[9], (D, FF), D ** -0.5, 0.125, ((0, 32),)),
        "w_down": scatter_about(key_of[10], (FF, D), FF ** -0.5, 0.0625, ((0, 32),)),
        "out_grad": scatter_about(key_of[11], (SEQS, LENGTH, D), 1.0, 6.0, ((0, 4), (1, 8))),
    }


eps = 1e-05
rope_base = 130000.0
mask_fill = -1e+30
highest = lax.Precision.HIGHEST

@jax.custom_vjp
def low(v):
    return lax.optimization_barrier(v.astype(jnp.bfloat16)).astype(jnp.float32)

@jax.custom_vjp
def low_back(v):
    return v

def low_keep(v):
    return (low(v), None)

def low_pass(kept, grad):
    return (grad,)

def back_keep(v):
    return (v, None)

def back_low(kept, grad):
    return (low(grad),)
low.defvjp(low_keep, low_pass)
low_back.defvjp(back_keep, back_low)

def rms_scale(values):
    return lax.rsqrt(lax.optimization_barrier(jnp.mean(values * values, axis=-1, keepdims=True)) + eps)

def angle_table(positions):
    exponents = jnp.arange(HEAD_DIM // 2, dtype=jnp.float32) * (2.0 / HEAD_DIM)
    inverse = jnp.exp(-math.log(rope_base) * exponents)
    return positions.astype(jnp.float32)[:, None, None] * inverse[None, None, :]

def rotate(values, angles):
    half_dim = values.shape[-1] // 2
    first_half = values[..., :half_dim]
    second_half = values[..., half_dim:]
    cosine = jnp.cos(angles)
    sine_part = jnp.sin(angles)
    return jnp.concatenate([first_half * cosine - second_half * sine_part, second_half * cosine + first_half * sine_part], axis=-1)

def attend(query_rot, key_rot, value_rows, positions):
    length = query_rot.shape[0]
    block_rows = math.gcd(length, 512)
    score_scale = 1.0 / math.sqrt(HEAD_DIM)
    query_blocks = query_rot.reshape(length // block_rows, block_rows, HEADS, HEAD_DIM)
    pos_blocks = positions.reshape(length // block_rows, block_rows)

    def one_block(block_members):
        query_block, pos_block = block_members
        scores = low_back(jnp.einsum('qhd,khd->hqk', query_block, key_rot, precision=highest) * score_scale)
        allowed = positions[None, None, :] <= pos_block[None, :, None]
        scores = jnp.where(allowed, scores, mask_fill)
        row_max = lax.optimization_barrier(jnp.max(scores, axis=-1, keepdims=True))
        weights = jnp.exp(scores - row_max)
        row_total = lax.optimization_barrier(jnp.sum(weights, axis=-1))
        mixed_rows = jnp.einsum('hqk,khd->qhd', low(weights), value_rows, precision=highest)
        return mixed_rows / jnp.transpose(row_total)[:, :, None]
    outputs = lax.map(jax.checkpoint(one_block), (query_blocks, pos_blocks))
    return outputs.reshape(length, HEADS * HEAD_DIM)

def block_forward(hidden, positions, attn_gain, w_query, w_key, w_value, w_out, mlp_gain, w_gate, w_up, w_down):
    row_count = hidden.shape[0]
    normed = low(hidden * rms_scale(hidden) * attn_gain)
    angles = angle_table(positions)

    def split_heads(values):
        return values.reshape(row_count, HEADS, HEAD_DIM)
    query_rot = low(rotate(split_heads(low_back(jnp.dot(normed, w_query, precision=highest))), angles))
    key_rot = low(rotate(split_heads(low_back(jnp.dot(normed, w_key, precision=highest))), angles))
    value_rows = split_heads(low_back(low(jnp.dot(normed, w_value, precision=highest))))
    attended = low_back(low(attend(query_rot, key_rot, value_rows, positions)))
    middle = hidden + low_back(jnp.dot(attended, w_out, precision=highest))
    normed_mid = low(middle * rms_scale(middle) * mlp_gain)
    gate_act = low_back(jnp.dot(normed_mid, w_gate, precision=highest))
    up_act = low_back(jnp.dot(normed_mid, w_up, precision=highest))
    inner_act = low(jax.nn.silu(gate_act) * up_act)
    return middle + jnp.dot(inner_act, w_down, precision=highest)

def reference(hidden_in, positions, attn_gain, w_query, w_key, w_value, w_out, mlp_gain, w_gate, w_up, w_down, out_grad):
    weights_in = tuple((member.astype(jnp.float32) for member in (attn_gain, w_query, w_key, w_value, w_out, mlp_gain, w_gate, w_up, w_down)))
    hidden = hidden_in.astype(jnp.float32)

    def forward(hidden_all, weight_set):

        def per_sequence(seq_members):
            seq_hidden, seq_pos = seq_members
            return block_forward(seq_hidden, seq_pos, weight_set[0], weight_set[1], weight_set[2], weight_set[3], weight_set[4], weight_set[5], weight_set[6], weight_set[7], weight_set[8])
        return lax.map(per_sequence, (hidden_all, positions))
    result, pullback = jax.vjp(forward, hidden, weights_in)
    hidden_grad, weight_grads = pullback(out_grad.astype(jnp.float32))
    return (result.astype(jnp.bfloat16), hidden_grad, weight_grads[0], weight_grads[1], weight_grads[2], weight_grads[3], weight_grads[4], weight_grads[5], weight_grads[6], weight_grads[7], weight_grads[8])
```

```python
import math

import jax
import jax.numpy as jnp
from jax import lax
from jax.sharding import PartitionSpec as P

HEADS = 32
HEAD_DIM = 64

eps = 1e-05
rope_base = 130000.0
mask_fill = -1e30
bf16 = jnp.bfloat16
f32 = jnp.float32


def gather_ctx(block):
    return lax.all_gather(block, "ctx", axis=0, tiled=True)


def gather_seq(block):
    return lax.all_gather(block, "seq", axis=0, tiled=True)


def scatter_ctx(total):
    return lax.psum_scatter(total.astype(bf16), "ctx", scatter_dimension=0, tiled=True).astype(f32)


def scatter_seq(total):
    return lax.psum_scatter(total.astype(bf16), "seq", scatter_dimension=0, tiled=True)


def swap_ctx(blocks):
    return lax.all_to_all(blocks, "ctx", 0, 0, tiled=True)


def rms_scale(values):
    return lax.rsqrt(jnp.mean(values * values, axis=-1, keepdims=True) + eps)


def angle_table(positions):
    exponents = jnp.arange(HEAD_DIM // 2, dtype=f32) * (2.0 / HEAD_DIM)
    inverse = jnp.exp(-math.log(rope_base) * exponents)
    return positions.astype(f32)[:, None, None] * inverse[None, None, :]


def rotate(values, cosine, sine_part):
    half_dim = HEAD_DIM // 2
    heads = values.reshape(values.shape[0], -1, HEAD_DIM)
    first_half = heads[..., :half_dim]
    second_half = heads[..., half_dim:]
    return jnp.concatenate(
        [
            first_half * cosine - second_half * sine_part,
            second_half * cosine + first_half * sine_part,
        ],
        axis=-1,
    ).reshape(values.shape)


def dot(left, right):
    return jnp.dot(left, right, preferred_element_type=f32)


def dot_rows(left, right):
    return lax.dot_general(left, right, (((0,), (0,)), ((), ())), preferred_element_type=f32)


def dot_cols(left, right):
    return lax.dot_general(left, right, (((1,), (1,)), ((), ())), preferred_element_type=f32)


def columns_to_owners(weight, groups):
    n = lax.axis_size("ctx")
    rows = weight.shape[0]
    width = weight.shape[1] // (n * groups)
    blocks = weight.reshape(rows, groups, n, width).transpose(2, 0, 1, 3)
    mine = swap_ctx(blocks.reshape(n, rows, groups * width))
    return gather_seq(mine.reshape(n * rows, groups * width))


def columns_from_owners(total, groups):
    n = lax.axis_size("ctx")
    part = scatter_seq(total)
    rows = part.shape[0] // n
    width = part.shape[1] // groups
    back = swap_ctx(part.reshape(n, rows, groups * width))
    back = back.reshape(n, rows, groups, width).transpose(1, 2, 0, 3)
    return back.reshape(rows, groups * n * width)


def attention(query, key, value, positions):
    heads = query.shape[1] // HEAD_DIM
    scale = 1.0 / math.sqrt(HEAD_DIM)
    allowed = positions[None, None, :] <= positions[None, :, None]
    qh, kh, vh = (m.reshape(-1, heads, HEAD_DIM) for m in (query, key, value))
    scores = jnp.einsum("qhd,khd->hqk", qh, kh, preferred_element_type=f32) * scale
    scores = jnp.where(allowed, scores, mask_fill)
    row_max = jnp.max(scores, axis=-1)
    weights = jnp.exp(scores - row_max[:, :, None])
    row_total = jnp.sum(weights, axis=-1)
    mixed = jnp.einsum("hqk,khd->qhd", weights.astype(bf16), vh, preferred_element_type=f32)
    attended = mixed / row_total.T[:, :, None]
    return attended.reshape(query.shape), row_max + jnp.log(row_total)


def attention_back(query, key, value, positions, attended, lse, grad):
    heads = query.shape[1] // HEAD_DIM
    scale = 1.0 / math.sqrt(HEAD_DIM)
    allowed = positions[None, None, :] <= positions[None, :, None]
    qh, kh, vh, gh = (m.reshape(-1, heads, HEAD_DIM) for m in (query, key, value, grad))
    row_delta = jnp.sum(gh.astype(f32) * attended.reshape(-1, heads, HEAD_DIM), axis=-1)
    scores = jnp.einsum("qhd,khd->hqk", qh, kh, preferred_element_type=f32) * scale
    prob = jnp.where(allowed, jnp.exp(scores - lse[:, :, None]), 0.0)
    prob_grad = jnp.einsum("qhd,khd->hqk", gh, vh, preferred_element_type=f32)
    score_grad = (prob * (prob_grad - row_delta.T[:, :, None])).astype(bf16)
    prob_low = prob.astype(bf16)
    value_acc = jnp.einsum("hqk,qhd->khd", prob_low, gh, preferred_element_type=f32)
    query_acc = jnp.einsum("hqk,khd->qhd", score_grad, kh, preferred_element_type=f32) * scale
    key_acc = jnp.einsum("hqk,qhd->khd", score_grad, qh, preferred_element_type=f32) * scale
    return tuple(m.reshape(query.shape) for m in (query_acc, key_acc, value_acc))


def local(
    hidden_in,
    positions,
    attn_gain,
    w_query,
    w_key,
    w_value,
    w_out,
    mlp_gain,
    w_gate,
    w_up,
    w_down,
    out_grad,
):
    n = lax.axis_size("ctx")
    seqs = lax.axis_size("seq")
    here = lax.axis_index("ctx")
    rows = hidden_in.shape[1]

    def own_rows(whole):
        return lax.dynamic_slice_in_dim(whole, here * rows, rows, 0)

    qkv_sub = columns_to_owners(jnp.concatenate([w_query, w_key, w_value], axis=1), 3)
    x_low = gather_ctx(hidden_in[0])
    pos_all = gather_ctx(positions[0])
    gains = lax.all_gather(jnp.stack([attn_gain, mlp_gain]), ("seq", "ctx"), axis=1, tiled=True)
    full_out = lax.all_gather(w_out, ("seq", "ctx"), axis=0, tiled=True)
    gate_up = columns_to_owners(jnp.concatenate([w_gate, w_up], axis=1), 2 * seqs)
    down_sub = gather_seq(w_down)
    grad_all = gather_ctx(out_grad[0])

    x = x_low.astype(f32)
    attn_scale = rms_scale(x)
    gain1 = gains[0].astype(f32)
    gain2 = gains[1].astype(f32)
    normed = (x * attn_scale * gain1).astype(bf16)
    angles = angle_table(pos_all)
    cosine, sine = jnp.cos(angles), jnp.sin(angles)
    qkv = dot(normed, qkv_sub)
    width = qkv.shape[1] // 3
    query = rotate(qkv[:, :width], cosine, sine).astype(bf16)
    key = rotate(qkv[:, width : 2 * width], cosine, sine).astype(bf16)
    value = qkv[:, 2 * width :].astype(bf16)
    attended, lse = attention(query, key, value, pos_all)
    att_low = lax.all_gather(attended.astype(bf16), "ctx", axis=1, tiled=True)

    middle = x + dot(att_low, full_out)
    mlp_scale = rms_scale(middle)
    normed_mid = (middle * mlp_scale * gain2).astype(bf16)
    gate_up_act = dot(normed_mid, gate_up)
    units = gate_up.shape[1] // 2
    gate_act, up_act = gate_up_act[:, :units], gate_up_act[:, units:]
    sig = jax.nn.sigmoid(gate_act)
    inner = (gate_act * sig * up_act).astype(bf16)
    middle_own = own_rows(middle)
    hidden_out = (middle_own + scatter_ctx(dot(inner, down_sub))).astype(bf16)

    inner_grad = dot_cols(grad_all, down_sub)
    gate_grad = (inner_grad * up_act * sig * (1.0 + gate_act * (1.0 - sig))).astype(bf16)
    up_grad = (inner_grad * gate_act * sig).astype(bf16)
    gate_up_grad = jnp.concatenate([gate_grad, up_grad], axis=1)
    mid_grad_in = scatter_ctx(dot_cols(gate_up_grad, gate_up))
    w_gate_up_grad = columns_from_owners(dot_rows(normed_mid, gate_up_grad), 2 * seqs).astype(f32)
    hidden_units = w_gate.shape[1]
    w_down_grad = scatter_seq(dot_rows(inner, grad_all)).astype(f32)

    mid_scale = own_rows(mlp_scale)
    mid_unit = middle_own * mid_scale
    mid_term = mid_grad_in * gain2
    middle_grad = out_grad[0].astype(f32) + mid_scale * (
        mid_term - mid_unit * jnp.mean(mid_unit * mid_term, axis=-1, keepdims=True)
    )
    mlp_gain_part = jnp.sum(mid_grad_in * mid_unit, axis=0)
    middle_low = middle_grad.astype(bf16)
    att_grad = dot_cols(middle_low, full_out).astype(bf16)
    att_grad = swap_ctx(att_grad.reshape(rows, n, -1).transpose(1, 0, 2)).reshape(n * rows, -1)
    middle_low_all = gather_ctx(middle_low)
    out_rows = w_out.shape[0]
    att_cols = att_low.reshape(n * rows, seqs, n, out_rows)
    att_sub = lax.dynamic_slice_in_dim(att_cols, here, 1, 2).reshape(n * rows, seqs * out_rows)
    w_out_grad = scatter_seq(dot_rows(att_sub, middle_low_all)).astype(f32)

    query_acc, key_acc, value_acc = attention_back(
        query, key, value, pos_all, attended, lse, att_grad
    )
    qkv_grad = jnp.concatenate(
        [rotate(query_acc, cosine, -sine), rotate(key_acc, cosine, -sine), value_acc], axis=1
    ).astype(bf16)
    normed_grad = scatter_ctx(dot_cols(qkv_grad, qkv_sub))
    own_scale = own_rows(attn_scale)
    own_unit = hidden_in[0].astype(f32) * own_scale
    attn_term = normed_grad * gain1
    hidden_grad = middle_grad + own_scale * (
        attn_term - own_unit * jnp.mean(own_unit * attn_term, axis=-1, keepdims=True)
    )
    attn_gain_part = jnp.sum(normed_grad * own_unit, axis=0)
    w_qkv_grad = columns_from_owners(dot_rows(normed, qkv_grad), 3).astype(f32)
    model_width = x.shape[1]
    gain_grads = lax.psum_scatter(
        jnp.stack([attn_gain_part, mlp_gain_part], axis=1),
        ("seq", "ctx"),
        scatter_dimension=0,
        tiled=True,
    )
    return (
        hidden_out[None],
        hidden_grad[None],
        gain_grads[:, 0],
        w_qkv_grad[:, :model_width],
        w_qkv_grad[:, model_width : 2 * model_width],
        w_qkv_grad[:, 2 * model_width :],
        w_out_grad,
        gain_grads[:, 1],
        w_gate_up_grad[:, :hidden_units],
        w_gate_up_grad[:, hidden_units:],
        w_down_grad,
    )


def solution(mesh):
    tokens = P("seq", "ctx", None)
    whole = P(("seq", "ctx"), None)
    gain = P(("seq", "ctx"))
    return jax.shard_map(
        local,
        mesh=mesh,
        in_specs=(
            tokens,
            P("seq", "ctx"),
            gain,
            whole,
            whole,
            whole,
            whole,
            gain,
            whole,
            whole,
            whole,
            tokens,
        ),
        out_specs=(tokens, tokens, gain, whole, whole, whole, whole, gain, whole, whole, whole),
        check_vma=False,
    )
```

```python
import math

import jax
import jax.numpy as jnp
from jax import lax
from jax.sharding import PartitionSpec as P

HEADS = 32
HEAD_DIM = 64

eps = 1e-05
rope_base = 130000.0
mask_fill = -1e30
bf16 = jnp.bfloat16
f32 = jnp.float32


def swap(block, axis, mask):
    n = lax.axis_size(axis)
    return lax.ppermute(block, axis, [(i, i ^ mask) for i in range(n)])


def ctx_masks():
    masks = []
    bit = lax.axis_size("ctx") // 2
    while bit:
        masks.append(bit ^ (bit >> 1) if bit > 2 else bit)
        bit //= 2
    return masks


def gather_ctx(block):
    held = [(0, block)]
    for mask in ctx_masks():
        held += [(offset ^ mask, swap(part, "ctx", mask)) for offset, part in held]
    return held


def gather_seq(block):
    held = [(0, block)]
    mask = lax.axis_size("seq") // 2
    while mask:
        held += [(offset ^ mask, swap(part, "seq", mask)) for offset, part in held]
        mask //= 2
    return held


def ordered(held, axis):
    here = lax.axis_index(axis)
    block = held[0][1]
    whole = jnp.zeros((len(held),) + block.shape, block.dtype)
    for offset, part in held:
        whole = lax.dynamic_update_index_in_dim(whole, part, here ^ offset, 0)
    return whole


def rows_of(held, axis):
    whole = ordered(held, axis)
    return whole.reshape((whole.shape[0] * whole.shape[1],) + whole.shape[2:])


def sum_over(parts, axis, masks):
    levels = [[0]]
    for mask in masks:
        levels.append([offset ^ mask for level in levels for offset in level])
    for mask, level in reversed(list(zip(masks, levels[1:]))):
        for offset in reversed(level):
            got = swap(parts.pop(offset).astype(bf16), axis, mask)
            parts[offset ^ mask] = parts[offset ^ mask].astype(f32) + got.astype(f32)
    return parts[0]


def scatter_ctx(total):
    n = lax.axis_size("ctx")
    here = lax.axis_index("ctx")
    rows = total.shape[0] // n
    parts = {
        o: lax.dynamic_slice_in_dim(total, (here ^ o) * rows, rows, 0) for o in range(n)
    }
    return sum_over(parts, "ctx", ctx_masks())


def scatter_seq(total):
    n = lax.axis_size("seq")
    here = lax.axis_index("seq")
    rows = total.shape[0] // n
    piece = lambda o: lax.dynamic_slice_in_dim(total, (here ^ o) * rows, rows, 0)
    got = swap(jnp.concatenate([piece(3), piece(1)], axis=0).astype(bf16), "seq", 1).astype(f32)
    far = swap((piece(2) + got[:rows]).astype(bf16), "seq", 2).astype(f32)
    return piece(0) + got[rows:] + far


def swap_ctx(block_of):
    n = lax.axis_size("ctx")
    here = lax.axis_index("ctx")
    return [(o, swap(block_of(here ^ o), "ctx", o) if o else block_of(here)) for o in range(n)]


def total_over_all(values):
    for axis in ("ctx", "seq"):
        mask = 1
        while mask < lax.axis_size(axis):
            values = values + swap(values, axis, mask)
            mask *= 2
    return values


def rms_scale(values):
    return lax.rsqrt(jnp.mean(values * values, axis=-1, keepdims=True) + eps)


def angle_table(positions):
    exponents = jnp.arange(HEAD_DIM // 2, dtype=f32) * (2.0 / HEAD_DIM)
    inverse = jnp.exp(-math.log(rope_base) * exponents)
    return positions.astype(f32)[:, None, None] * inverse[None, None, :]


def rotate(values, cosine, sine_part):
    half_dim = HEAD_DIM // 2
    heads = values.reshape(values.shape[0], -1, HEAD_DIM)
    first_half = heads[..., :half_dim]
    second_half = heads[..., half_dim:]
    return jnp.concatenate(
        [
            first_half * cosine - second_half * sine_part,
            second_half * cosine + first_half * sine_part,
        ],
        axis=-1,
    ).reshape(values.shape)


def dot(left, right):
    return jnp.dot(left, right, preferred_element_type=f32)


def dot_rows(left, right):
    return lax.dot_general(left, right, (((0,), (0,)), ((), ())), preferred_element_type=f32)


def dot_cols(left, right):
    return lax.dot_general(left, right, (((1,), (1,)), ((), ())), preferred_element_type=f32)


def columns_to_owners(weights, groups):
    n = lax.axis_size("ctx")
    rows = weights[0].shape[0]
    width = weights[0].shape[1] // (n * groups)

    def block_of(device):
        cuts = [
            lax.dynamic_slice_in_dim(weight, (g * n + device) * width, width, 1)
            for weight in weights
            for g in range(groups)
        ]
        return jnp.concatenate(cuts, axis=1)

    mine = rows_of(swap_ctx(block_of), "ctx")
    return rows_of(gather_seq(mine), "seq")


def columns_from_owners(total, count, groups):
    n = lax.axis_size("ctx")
    part = scatter_seq(total).astype(bf16)
    rows = part.shape[0] // n
    width = part.shape[1] // (count * groups)
    back = swap_ctx(lambda device: lax.dynamic_slice_in_dim(part, device * rows, rows, 0))
    back = ordered(back, "ctx").reshape(n, rows, count, groups, width)
    return [
        back[:, :, i].transpose(1, 2, 0, 3).reshape(rows, groups * n * width).astype(f32)
        for i in range(count)
    ]


def attention(query, key, value, positions):
    heads = query.shape[1] // HEAD_DIM
    scale = 1.0 / math.sqrt(HEAD_DIM)
    allowed = positions[None, None, :] <= positions[None, :, None]
    qh, kh, vh = (m.reshape(-1, heads, HEAD_DIM) for m in (query, key, value))
    scores = jnp.einsum("qhd,khd->hqk", qh, kh, preferred_element_type=f32) * scale
    scores = jnp.where(allowed, scores, mask_fill)
    row_max = jnp.max(scores, axis=-1)
    weights = jnp.exp(scores - row_max[:, :, None])
    row_total = jnp.sum(weights, axis=-1)
    mixed = jnp.einsum("hqk,khd->qhd", weights.astype(bf16), vh, preferred_element_type=f32)
    attended = mixed / row_total.T[:, :, None]
    return attended.reshape(query.shape), row_max + jnp.log(row_total)


def attention_back(query, key, value, positions, attended, lse, grad):
    heads = query.shape[1] // HEAD_DIM
    scale = 1.0 / math.sqrt(HEAD_DIM)
    allowed = positions[None, None, :] <= positions[None, :, None]
    qh, kh, vh, gh = (m.reshape(-1, heads, HEAD_DIM) for m in (query, key, value, grad))
    row_delta = jnp.sum(gh.astype(f32) * attended.reshape(-1, heads, HEAD_DIM), axis=-1)
    scores = jnp.einsum("qhd,khd->hqk", qh, kh, preferred_element_type=f32) * scale
    prob = jnp.where(allowed, jnp.exp(scores - lse[:, :, None]), 0.0)
    prob_grad = jnp.einsum("qhd,khd->hqk", gh, vh, preferred_element_type=f32)
    score_grad = (prob * (prob_grad - row_delta.T[:, :, None])).astype(bf16)
    prob_low = prob.astype(bf16)
    value_acc = jnp.einsum("hqk,qhd->khd", prob_low, gh, preferred_element_type=f32)
    query_acc = jnp.einsum("hqk,khd->qhd", score_grad, kh, preferred_element_type=f32) * scale
    key_acc = jnp.einsum("hqk,qhd->khd", score_grad, qh, preferred_element_type=f32) * scale
    return tuple(m.reshape(query.shape) for m in (query_acc, key_acc, value_acc))


def local(
    hidden_in,
    positions,
    attn_gain,
    w_query,
    w_key,
    w_value,
    w_out,
    mlp_gain,
    w_gate,
    w_up,
    w_down,
    out_grad,
):
    n = lax.axis_size("ctx")
    seqs = lax.axis_size("seq")
    here = lax.axis_index("ctx")
    rows = hidden_in.shape[1]

    def own_rows(whole):
        return lax.dynamic_slice_in_dim(whole, here * rows, rows, 0)

    pos_high, pos_low = positions[0] // 64, positions[0] % 64
    small = jnp.concatenate(
        [pos_high.astype(bf16), pos_low.astype(bf16), attn_gain, mlp_gain]
    ).reshape(1, -1)
    small = rows_of(gather_ctx(small), "ctx")
    pos_all = (small[:, :rows].astype(jnp.int32) * 64 + small[:, rows : 2 * rows].astype(jnp.int32)).reshape(-1)
    gains = ordered(gather_seq(small[:, 2 * rows :]), "seq").reshape(seqs, n, 2, -1)
    gain1 = gains[:, :, 0].reshape(-1).astype(f32)
    gain2 = gains[:, :, 1].reshape(-1).astype(f32)
    x_low = rows_of(gather_ctx(hidden_in[0]), "ctx")
    qkv_sub = columns_to_owners((w_query, w_key, w_value), 1)
    down_sub = rows_of(gather_seq(w_down), "seq")
    grad_all = rows_of(gather_ctx(out_grad[0]), "ctx")
    full_out = lax.all_gather(w_out, ("seq", "ctx"), axis=0, tiled=True)
    gate_sub = columns_to_owners((w_gate,), seqs)
    up_sub = columns_to_owners((w_up,), seqs)

    x = x_low.astype(f32)
    attn_scale = rms_scale(x)
    normed = (x * attn_scale * gain1).astype(bf16)
    angles = angle_table(pos_all)
    cosine, sine = jnp.cos(angles), jnp.sin(angles)
    qkv = dot(normed, qkv_sub)
    width = qkv.shape[1] // 3
    query = rotate(qkv[:, :width], cosine, sine).astype(bf16)
    key = rotate(qkv[:, width : 2 * width], cosine, sine).astype(bf16)
    value = qkv[:, 2 * width :].astype(bf16)
    attended, lse = attention(query, key, value, pos_all)
    att_low = ordered(gather_ctx(attended.astype(bf16)), "ctx")
    att_low = att_low.transpose(1, 0, 2).reshape(n * rows, -1)

    middle = x + dot(att_low, full_out)
    mlp_scale = rms_scale(middle)
    normed_mid = (middle * mlp_scale * gain2).astype(bf16)
    gate_act = dot(normed_mid, gate_sub)
    up_act = dot(normed_mid, up_sub)
    sig = jax.nn.sigmoid(gate_act)
    inner = (gate_act * sig * up_act).astype(bf16)
    middle_own = own_rows(middle)
    hidden_out = (middle_own + scatter_ctx(dot(inner, down_sub))).astype(bf16)

    inner_grad = dot_cols(grad_all, down_sub)
    gate_grad = (inner_grad * up_act * sig * (1.0 + gate_act * (1.0 - sig))).astype(bf16)
    up_grad = (inner_grad * gate_act * sig).astype(bf16)
    mid_grad_in = scatter_ctx(dot_cols(gate_grad, gate_sub) + dot_cols(up_grad, up_sub))
    (w_gate_grad,) = columns_from_owners(dot_rows(normed_mid, gate_grad), 1, seqs)
    (w_up_grad,) = columns_from_owners(dot_rows(normed_mid, up_grad), 1, seqs)
    w_down_grad = scatter_seq(dot_rows(inner, grad_all))

    mid_scale = own_rows(mlp_scale)
    mid_unit = middle_own * mid_scale
    mid_term = mid_grad_in * gain2
    middle_grad = out_grad[0].astype(f32) + mid_scale * (
        mid_term - mid_unit * jnp.mean(mid_unit * mid_term, axis=-1, keepdims=True)
    )
    mlp_gain_part = jnp.sum(mid_grad_in * mid_unit, axis=0)
    middle_low = middle_grad.astype(bf16)
    att_grad_own = dot_cols(middle_low, full_out).astype(bf16)
    head_cols = att_grad_own.shape[1] // n
    att_grad = rows_of(
        swap_ctx(lambda d: lax.dynamic_slice_in_dim(att_grad_own, d * head_cols, head_cols, 1)), "ctx"
    )
    middle_low_all = rows_of(gather_ctx(middle_low), "ctx")
    out_rows = w_out.shape[0]
    att_cols = att_low.reshape(n * rows, seqs, n, out_rows)
    att_sub = lax.dynamic_slice_in_dim(att_cols, here, 1, 2).reshape(n * rows, seqs * out_rows)
    w_out_grad = scatter_seq(dot_rows(att_sub, middle_low_all))

    query_acc, key_acc, value_acc = attention_back(
        query, key, value, pos_all, attended, lse, att_grad
    )
    qkv_grad = jnp.concatenate(
        [rotate(query_acc, cosine, -sine), rotate(key_acc, cosine, -sine), value_acc], axis=1
    ).astype(bf16)
    normed_grad_part = dot_cols(qkv_grad, qkv_sub)
    attn_gain_part = jnp.sum(normed_grad_part * (x * attn_scale), axis=0)
    gain_grads = total_over_all(jnp.stack([attn_gain_part, mlp_gain_part]))
    gain_rows = attn_gain.shape[0]
    place = (lax.axis_index("seq") * n + here) * gain_rows
    gain_grads = lax.dynamic_slice_in_dim(gain_grads, place, gain_rows, 1)
    normed_grad = scatter_ctx(normed_grad_part)
    own_scale = own_rows(attn_scale)
    own_unit = hidden_in[0].astype(f32) * own_scale
    attn_term = normed_grad * gain1
    hidden_grad = middle_grad + own_scale * (
        attn_term - own_unit * jnp.mean(own_unit * attn_term, axis=-1, keepdims=True)
    )
    w_query_grad, w_key_grad, w_value_grad = columns_from_owners(dot_rows(normed, qkv_grad), 3, 1)
    return (
        hidden_out[None],
        hidden_grad[None],
        gain_grads[0],
        w_query_grad,
        w_key_grad,
        w_value_grad,
        w_out_grad,
        gain_grads[1],
        w_gate_grad,
        w_up_grad,
        w_down_grad,
    )


def solution(mesh):
    tokens = P("seq", "ctx", None)
    whole = P(("seq", "ctx"), None)
    gain = P(("seq", "ctx"))
    return jax.shard_map(
        local,
        mesh=mesh,
        in_specs=(
            tokens,
            P("seq", "ctx"),
            gain,
            whole,
            whole,
            whole,
            whole,
            gain,
            whole,
            whole,
            whole,
            tokens,
        ),
        out_specs=(tokens, tokens, gain, whole, whole, whole, whole, gain, whole, whole, whole),
        check_vma=False,
    )
```

```python
import math

import jax
import jax.numpy as jnp
from jax import lax
from jax.experimental import pallas as pl
from jax.experimental.pallas import tpu as pltpu
from jax.sharding import PartitionSpec as P

HEADS = 32
HEAD_DIM = 64

eps = 1e-05
rope_base = 130000.0
mask_fill = -1e30
bf16 = jnp.bfloat16
f32 = jnp.float32


def plain_gather_ctx(block):
    return lax.all_gather(block, "ctx", axis=0, tiled=True)


def plain_gather_seq(block):
    return lax.all_gather(block, "seq", axis=0, tiled=True)


def plain_scatter_ctx(total):
    return lax.psum_scatter(total.astype(bf16), "ctx", scatter_dimension=0, tiled=True).astype(f32)


def plain_scatter_seq(total):
    return lax.psum_scatter(total.astype(bf16), "seq", scatter_dimension=0, tiled=True)


def plain_swap_ctx(blocks):
    return lax.all_to_all(blocks, "ctx", 0, 0, tiled=True)


def rms_scale(values):
    return lax.rsqrt(jnp.mean(values * values, axis=-1, keepdims=True) + eps)


def angle_table(positions):
    exponents = jnp.arange(HEAD_DIM // 2, dtype=f32) * (2.0 / HEAD_DIM)
    inverse = jnp.exp(-math.log(rope_base) * exponents)
    return positions.astype(f32)[:, None, None] * inverse[None, None, :]


def rotate(values, cosine, sine_part):
    half_dim = HEAD_DIM // 2
    heads = values.reshape(values.shape[0], -1, HEAD_DIM)
    first_half = heads[..., :half_dim]
    second_half = heads[..., half_dim:]
    return jnp.concatenate(
        [
            first_half * cosine - second_half * sine_part,
            second_half * cosine + first_half * sine_part,
        ],
        axis=-1,
    ).reshape(values.shape)


def dot(left, right):
    return jnp.dot(left, right, preferred_element_type=f32)


def dot_rows(left, right):
    return lax.dot_general(left, right, (((0,), (0,)), ((), ())), preferred_element_type=f32)


def dot_cols(left, right):
    return lax.dot_general(left, right, (((1,), (1,)), ((), ())), preferred_element_type=f32)


def columns_to_owners(weight, groups):
    n = lax.axis_size("ctx")
    rows = weight.shape[0]
    width = weight.shape[1] // (n * groups)
    blocks = weight.reshape(rows, groups, n, width).transpose(2, 0, 1, 3)
    mine = plain_swap_ctx(blocks.reshape(n, rows, groups * width))
    return plain_gather_seq(mine.reshape(n * rows, groups * width))


def columns_from_owners(total, groups):
    n = lax.axis_size("ctx")
    part = plain_scatter_seq(total)
    rows = part.shape[0] // n
    width = part.shape[1] // groups
    back = plain_swap_ctx(part.reshape(n, rows, groups * width))
    back = back.reshape(n, rows, groups, width).transpose(1, 2, 0, 3)
    return back.reshape(rows, groups * n * width)


def attention(query, key, value, positions):
    heads = query.shape[1] // HEAD_DIM
    scale = 1.0 / math.sqrt(HEAD_DIM)
    allowed = positions[None, None, :] <= positions[None, :, None]
    qh, kh, vh = (m.reshape(-1, heads, HEAD_DIM) for m in (query, key, value))
    scores = jnp.einsum("qhd,khd->hqk", qh, kh, preferred_element_type=f32) * scale
    scores = jnp.where(allowed, scores, mask_fill)
    row_max = jnp.max(scores, axis=-1)
    weights = jnp.exp(scores - row_max[:, :, None])
    row_total = jnp.sum(weights, axis=-1)
    mixed = jnp.einsum("hqk,khd->qhd", weights.astype(bf16), vh, preferred_element_type=f32)
    attended = mixed / row_total.T[:, :, None]
    return attended.reshape(query.shape), row_max + jnp.log(row_total)


def attention_back(query, key, value, positions, attended, lse, grad):
    heads = query.shape[1] // HEAD_DIM
    scale = 1.0 / math.sqrt(HEAD_DIM)
    allowed = positions[None, None, :] <= positions[None, :, None]
    qh, kh, vh, gh = (m.reshape(-1, heads, HEAD_DIM) for m in (query, key, value, grad))
    row_delta = jnp.sum(gh.astype(f32) * attended.reshape(-1, heads, HEAD_DIM), axis=-1)
    scores = jnp.einsum("qhd,khd->hqk", qh, kh, preferred_element_type=f32) * scale
    prob = jnp.where(allowed, jnp.exp(scores - lse[:, :, None]), 0.0)
    prob_grad = jnp.einsum("qhd,khd->hqk", gh, vh, preferred_element_type=f32)
    score_grad = (prob * (prob_grad - row_delta.T[:, :, None])).astype(bf16)
    prob_low = prob.astype(bf16)
    value_acc = jnp.einsum("hqk,qhd->khd", prob_low, gh, preferred_element_type=f32)
    query_acc = jnp.einsum("hqk,khd->qhd", score_grad, kh, preferred_element_type=f32) * scale
    key_acc = jnp.einsum("hqk,qhd->khd", score_grad, qh, preferred_element_type=f32) * scale
    return tuple(m.reshape(query.shape) for m in (query_acc, key_acc, value_acc))


def plain(
    hidden_in,
    positions,
    attn_gain,
    w_query,
    w_key,
    w_value,
    w_out,
    mlp_gain,
    w_gate,
    w_up,
    w_down,
    out_grad,
):
    n = lax.axis_size("ctx")
    seqs = lax.axis_size("seq")
    here = lax.axis_index("ctx")
    rows = hidden_in.shape[1]

    def own_rows(whole):
        return lax.dynamic_slice_in_dim(whole, here * rows, rows, 0)

    qkv_sub = columns_to_owners(jnp.concatenate([w_query, w_key, w_value], axis=1), 3)
    x_low = plain_gather_ctx(hidden_in[0])
    pos_all = plain_gather_ctx(positions[0])
    gains = lax.all_gather(jnp.stack([attn_gain, mlp_gain]), ("seq", "ctx"), axis=1, tiled=True)
    full_out = lax.all_gather(w_out, ("seq", "ctx"), axis=0, tiled=True)
    gate_up = columns_to_owners(jnp.concatenate([w_gate, w_up], axis=1), 2 * seqs)
    down_sub = plain_gather_seq(w_down)
    grad_all = plain_gather_ctx(out_grad[0])

    x = x_low.astype(f32)
    attn_scale = rms_scale(x)
    gain1 = gains[0].astype(f32)
    gain2 = gains[1].astype(f32)
    normed = (x * attn_scale * gain1).astype(bf16)
    angles = angle_table(pos_all)
    cosine, sine = jnp.cos(angles), jnp.sin(angles)
    qkv = dot(normed, qkv_sub)
    width = qkv.shape[1] // 3
    query = rotate(qkv[:, :width], cosine, sine).astype(bf16)
    key = rotate(qkv[:, width : 2 * width], cosine, sine).astype(bf16)
    value = qkv[:, 2 * width :].astype(bf16)
    attended, lse = attention(query, key, value, pos_all)
    att_low = lax.all_gather(attended.astype(bf16), "ctx", axis=1, tiled=True)

    middle = x + dot(att_low, full_out)
    mlp_scale = rms_scale(middle)
    normed_mid = (middle * mlp_scale * gain2).astype(bf16)
    gate_up_act = dot(normed_mid, gate_up)
    units = gate_up.shape[1] // 2
    gate_act, up_act = gate_up_act[:, :units], gate_up_act[:, units:]
    sig = jax.nn.sigmoid(gate_act)
    inner = (gate_act * sig * up_act).astype(bf16)
    middle_own = own_rows(middle)
    hidden_out = (middle_own + plain_scatter_ctx(dot(inner, down_sub))).astype(bf16)

    inner_grad = dot_cols(grad_all, down_sub)
    gate_grad = (inner_grad * up_act * sig * (1.0 + gate_act * (1.0 - sig))).astype(bf16)
    up_grad = (inner_grad * gate_act * sig).astype(bf16)
    gate_up_grad = jnp.concatenate([gate_grad, up_grad], axis=1)
    mid_grad_in = plain_scatter_ctx(dot_cols(gate_up_grad, gate_up))
    w_gate_up_grad = columns_from_owners(dot_rows(normed_mid, gate_up_grad), 2 * seqs).astype(f32)
    hidden_units = w_gate.shape[1]
    w_down_grad = plain_scatter_seq(dot_rows(inner, grad_all)).astype(f32)

    mid_scale = own_rows(mlp_scale)
    mid_unit = middle_own * mid_scale
    mid_term = mid_grad_in * gain2
    middle_grad = out_grad[0].astype(f32) + mid_scale * (
        mid_term - mid_unit * jnp.mean(mid_unit * mid_term, axis=-1, keepdims=True)
    )
    mlp_gain_part = jnp.sum(mid_grad_in * mid_unit, axis=0)
    middle_low = middle_grad.astype(bf16)
    att_grad = dot_cols(middle_low, full_out).astype(bf16)
    att_grad = plain_swap_ctx(att_grad.reshape(rows, n, -1).transpose(1, 0, 2)).reshape(n * rows, -1)
    middle_low_all = plain_gather_ctx(middle_low)
    out_rows = w_out.shape[0]
    att_cols = att_low.reshape(n * rows, seqs, n, out_rows)
    att_sub = lax.dynamic_slice_in_dim(att_cols, here, 1, 2).reshape(n * rows, seqs * out_rows)
    w_out_grad = plain_scatter_seq(dot_rows(att_sub, middle_low_all)).astype(f32)

    query_acc, key_acc, value_acc = attention_back(
        query, key, value, pos_all, attended, lse, att_grad
    )
    qkv_grad = jnp.concatenate(
        [rotate(query_acc, cosine, -sine), rotate(key_acc, cosine, -sine), value_acc], axis=1
    ).astype(bf16)
    normed_grad = plain_scatter_ctx(dot_cols(qkv_grad, qkv_sub))
    own_scale = own_rows(attn_scale)
    own_unit = hidden_in[0].astype(f32) * own_scale
    attn_term = normed_grad * gain1
    hidden_grad = middle_grad + own_scale * (
        attn_term - own_unit * jnp.mean(own_unit * attn_term, axis=-1, keepdims=True)
    )
    attn_gain_part = jnp.sum(normed_grad * own_unit, axis=0)
    w_qkv_grad = columns_from_owners(dot_rows(normed, qkv_grad), 3).astype(f32)
    model_width = x.shape[1]
    gain_grads = lax.psum_scatter(
        jnp.stack([attn_gain_part, mlp_gain_part], axis=1),
        ("seq", "ctx"),
        scatter_dimension=0,
        tiled=True,
    )
    return (
        hidden_out[None],
        hidden_grad[None],
        gain_grads[:, 0],
        w_qkv_grad[:, :model_width],
        w_qkv_grad[:, model_width : 2 * model_width],
        w_qkv_grad[:, 2 * model_width :],
        w_out_grad,
        gain_grads[:, 1],
        w_gate_up_grad[:, :hidden_units],
        w_gate_up_grad[:, hidden_units:],
        w_down_grad,
    )


class Box:
    def __init__(self, value):
        self.value = value


def value_of(block):
    return block.value if isinstance(block, Box) else block


def order(block, *boxes):
    values = lax.optimization_barrier((value_of(block),) + tuple(box.value for box in boxes))
    for box, value in zip(boxes, values[1:]):
        box.value = value
    return values[0]


class Link:
    def __init__(self, axis, depth):
        self.axis = axis
        self.depth = depth
        self.arrived = []

    def swap(self, block, mask):
        n = lax.axis_size(self.axis)
        if len(self.arrived) >= self.depth:
            before = order(block, self.arrived[-self.depth])
            if isinstance(block, Box):
                block.value = before
            block = before
        got = Box(lax.ppermute(value_of(block), self.axis, [(i, i ^ mask) for i in range(n)]))
        self.arrived.append(got)
        return got


def place(pieces, places, columns=False):
    pieces = [value_of(piece) for piece in pieces]
    rows, width = pieces[0].shape
    count = len(pieces)
    shape = (rows, count * width) if columns else (count * rows, width)

    def kernel(places_ref, *refs):
        parts, whole, sems = refs[:count], refs[count], refs[count + 1]
        copies = []
        for i in range(count):
            if columns:
                there = whole.at[:, pl.ds(pl.multiple_of(places_ref[i] * width, width), width)]
            else:
                there = whole.at[pl.ds(pl.multiple_of(places_ref[i] * rows, rows), rows), :]
            copies.append(pltpu.make_async_copy(parts[i], there, sems.at[i]))
        for copy in copies:
            copy.start()
        for copy in copies:
            copy.wait()

    return pl.pallas_call(
        kernel,
        out_shape=jax.ShapeDtypeStruct(shape, pieces[0].dtype),
        in_specs=[pl.BlockSpec(memory_space=pltpu.SMEM)]
        + [pl.BlockSpec(memory_space=pl.ANY)] * count,
        out_specs=pl.BlockSpec(memory_space=pltpu.VMEM),
        scratch_shapes=[pltpu.SemaphoreType.DMA((count,))],
        compiler_params=pltpu.CompilerParams(vmem_limit_bytes=32 * 1024 * 1024),
        cost_estimate=pl.CostEstimate(flops=0, bytes_accessed=4 * rows * width * count, transcendentals=0),
    )(jnp.stack(places).astype(jnp.int32), *pieces)


def cut_columns(weights, groups, beside):
    n = lax.axis_size("ctx")
    rows = weights[0].shape[0]
    width = weights[0].shape[1] // (n * groups)
    arrays = list(weights) + ([] if beside is None else [beside])
    total = len(weights) * groups * width + (0 if beside is None else beside.shape[1])

    def kernel(*refs):
        out = refs[-1]
        for device in range(n):
            at = 0
            for weight in refs[: len(weights)]:
                for group in range(groups):
                    start = (group * n + device) * width
                    out[device, :, at : at + width] = weight[:, start : start + width]
                    at += width
            if beside is not None:
                out[device, :, at:] = refs[len(weights)][...]

    vmem = pl.BlockSpec(memory_space=pltpu.VMEM)
    return pl.pallas_call(
        kernel,
        out_shape=jax.ShapeDtypeStruct((n, rows, total), bf16),
        in_specs=[vmem] * len(arrays),
        out_specs=vmem,
        compiler_params=pltpu.CompilerParams(vmem_limit_bytes=32 * 1024 * 1024),
    )(*arrays)


def paste_columns(blocks, count, groups, beside=0):
    n, rows, total = blocks.shape
    width = (total - beside) // (count * groups)
    shapes = [jax.ShapeDtypeStruct((rows, groups * n * width), f32)] * count
    if beside:
        shapes.append(jax.ShapeDtypeStruct((rows, n * beside), f32))

    def kernel(ref, *outs):
        for device in range(n):
            at = 0
            for i in range(count):
                for group in range(groups):
                    start = (group * n + device) * width
                    outs[i][:, start : start + width] = ref[device, :, at : at + width].astype(f32)
                    at += width
            if beside:
                start = device * beside
                outs[count][:, start : start + beside] = ref[device, :, at:].astype(f32)

    vmem = pl.BlockSpec(memory_space=pltpu.VMEM)
    return pl.pallas_call(
        kernel,
        out_shape=shapes,
        in_specs=[vmem],
        out_specs=[vmem] * len(shapes),
        compiler_params=pltpu.CompilerParams(vmem_limit_bytes=32 * 1024 * 1024),
    )(blocks)


def gather_ctx(y, z, block):
    two = z.swap(block, 2)
    six = z.swap(block, 6)
    one = y.swap(block, 1)
    four = z.swap(six, 2)
    held = [(0, block), (2, two), (6, six), (1, one), (4, four)]
    for offset, part in ((3, two), (7, six), (5, four)):
        held.append((offset, y.swap(part, 1)))
    return held


def gather_seq(x, here, block):
    near = x.swap(block, 1)
    far = x.swap(block, 2)
    both = x.swap(far, 1)
    return [(0, block), (1, near), (2, far), (3, both)]


def scatter_ctx(y, z, total, here, beside=()):
    beside = list(beside)

    def after_next(block):
        return order(block, *beside.pop(0)()) if beside else block

    n = lax.axis_size("ctx")
    rows = total.shape[0] // n
    part = [lax.dynamic_slice_in_dim(total, (here ^ o) * rows, rows, 0) for o in range(n)]

    def add(offset, got):
        return part[offset].astype(f32) + got.value.astype(f32)

    four = add(4, y.swap(part[5], 1))
    two = add(2, y.swap(part[3], 1))
    got_four = z.swap(four.astype(bf16), 2)
    six = add(6, y.swap(after_next(part[7]), 1))
    got_two = z.swap(two.astype(bf16), 2)
    from_y = y.swap(part[1], 1)
    got_six = z.swap(after_next((six + got_four.value.astype(f32)).astype(bf16)), 6)
    return add(0, from_y) + got_two.value.astype(f32) + got_six.value.astype(f32)


def scatter_ctx_grouped(y, z, total, here):
    n = lax.axis_size("ctx")
    rows = total.shape[0] // n
    offsets = [0, 6, 2, 4, 1, 7, 3, 5]
    left = [lax.dynamic_slice_in_dim(total, (here ^ o) * rows, rows, 0) for o in offsets]
    for link, mask in ((y, 1), (z, 2), (z, 6)):
        half = len(left) // 2
        got = link.swap(jnp.concatenate(left[half:], axis=0).astype(bf16), mask)
        left = [
            part + got.value[i * rows : (i + 1) * rows].astype(f32)
            for i, part in enumerate(left[:half])
        ]
    return left[0]


def scatter_seq_near(x, total, here):
    rows = total.shape[0] // 4

    def piece(offset):
        return lax.dynamic_slice_in_dim(total, (here ^ offset) * rows, rows, 0)

    got = x.swap(jnp.concatenate([piece(3), piece(1)], axis=0).astype(bf16), 1)
    return piece(0) + got.value[rows:].astype(f32), (
        piece(2) + got.value[:rows].astype(f32)
    ).astype(bf16)


def to_owners(part, count, groups, beside=0):
    n = lax.axis_size("ctx")
    blocks = lax.all_to_all(part.reshape(n, -1, part.shape[1]), "ctx", 0, 0, tiled=True)
    return paste_columns(blocks, count, groups, beside)


def scatter_halves(y, z, total, here, beside=()):
    n = lax.axis_size("ctx")
    parts = total.reshape(n, 2, -1, total.shape[1])
    first = lax.psum_scatter(
        parts[:, 0].reshape(-1, total.shape[1]), "ctx", scatter_dimension=0, tiled=True
    )
    second = scatter_ctx(y, z, parts[:, 1].reshape(-1, total.shape[1]), here, beside)
    return jnp.concatenate([first.astype(f32), second], axis=0)


def tuned(
    hidden_in,
    positions,
    attn_gain,
    w_query,
    w_key,
    w_value,
    w_out,
    mlp_gain,
    w_gate,
    w_up,
    w_down,
    out_grad,
):
    n = lax.axis_size("ctx")
    seqs = lax.axis_size("seq")
    here = lax.axis_index("ctx")
    seq_here = lax.axis_index("seq")
    rows = hidden_in.shape[1]
    weight_rows = w_query.shape[0]
    y, z, x = Link("ctx", 2), Link("ctx", 2), Link("seq", 1)

    def own_rows(whole):
        return lax.dynamic_slice_in_dim(whole, here * rows, rows, 0)

    def from_devices(held, index=here):
        return place([part for _, part in held], [index ^ o for o, _ in held])

    own_pos = positions[0].reshape(weight_rows, -1)
    per_row = own_pos.shape[1]
    beside = jnp.concatenate(
        [
            attn_gain[:, None],
            mlp_gain[:, None],
            (own_pos // 64).astype(bf16),
            (own_pos % 64).astype(bf16),
        ],
        axis=1,
    )
    beside = jnp.pad(beside, ((0, 0), (0, 128 - beside.shape[1])))
    x_low = lax.all_gather(hidden_in[0], "ctx", axis=0, tiled=True)
    blocks = cut_columns((w_query, w_key, w_value), 1, beside)
    qkv_mine = lax.all_to_all(blocks, "ctx", 0, 0, tiled=True).reshape(n * weight_rows, -1)
    late_gate, late_up, late_out, late_down, qkv_mine = lax.optimization_barrier(
        (w_gate, w_up, w_out, w_down, qkv_mine)
    )
    full_out = lax.all_gather(late_out, ("seq", "ctx"), axis=0, tiled=True)
    qkv_steps = gather_seq(x, seq_here, qkv_mine)
    down_steps = gather_seq(x, seq_here, late_down)
    blocks = cut_columns((late_gate, late_up), seqs, None)
    gate_up = lax.all_to_all(blocks, "ctx", 0, 0, tiled=True).reshape(n * weight_rows, -1)
    gate_up_steps = gather_seq(x, seq_here, gate_up)
    qkv_sub = from_devices(qkv_steps, seq_here)
    down_sub = from_devices(down_steps, seq_here)
    gate_up = from_devices(gate_up_steps, seq_here)
    pos_cuts = qkv_mine[:, -128:].astype(jnp.int32)
    pos_all = pos_cuts[:, 2 : 2 + per_row] * 64 + pos_cuts[:, 2 + per_row : 2 + 2 * per_row]
    pos_all = pos_all.reshape(-1)
    gain1 = qkv_sub[:, -128].astype(f32)
    gain2 = qkv_sub[:, -127].astype(f32)
    qkv_sub = qkv_sub[:, :-128]

    x_all = x_low.astype(f32)
    attn_scale = rms_scale(x_all)
    normed = (x_all * attn_scale * gain1).astype(bf16)
    angles = angle_table(pos_all)
    cosine, sine = jnp.cos(angles), jnp.sin(angles)
    qkv = dot(normed, qkv_sub)
    width = qkv.shape[1] // 3
    query = rotate(qkv[:, :width], cosine, sine).astype(bf16)
    key = rotate(qkv[:, width : 2 * width], cosine, sine).astype(bf16)
    value = qkv[:, 2 * width :].astype(bf16)
    attended, lse = attention(query, key, value, pos_all)
    att_held = gather_ctx(y, z, attended.astype(bf16))
    att_low = place([part for _, part in att_held], [here ^ o for o, _ in att_held], columns=True)
    late_grad, att_low = lax.optimization_barrier((out_grad[0], att_low))
    grad_all = lax.all_gather(late_grad, "ctx", axis=0, tiled=True)

    middle = x_all + dot(att_low, full_out)
    mlp_scale = rms_scale(middle)
    normed_mid = (middle * mlp_scale * gain2).astype(bf16)
    gate_up_act = dot(normed_mid, gate_up)
    units = gate_up.shape[1] // 2
    gate_act, up_act = gate_up_act[:, :units], gate_up_act[:, units:]
    sig = jax.nn.sigmoid(gate_act)
    inner = (gate_act * sig * up_act).astype(bf16)
    middle_own = own_rows(middle)

    inner_grad = dot_cols(grad_all, down_sub)
    gate_grad = (inner_grad * up_act * sig * (1.0 + gate_act * (1.0 - sig))).astype(bf16)
    up_grad = (inner_grad * gate_act * sig).astype(bf16)
    gate_up_grad = jnp.concatenate([gate_grad, up_grad], axis=1)
    mid_grad_part = dot_cols(gate_up_grad, gate_up).astype(bf16)
    gate_up_near, gate_up_far = scatter_seq_near(x, dot_rows(normed_mid, gate_up_grad), seq_here)
    gate_up_far = Box(gate_up_far)
    mid_grad_in = scatter_halves(y, z, mid_grad_part, here, [lambda: [gate_up_far]])
    gate_up_far = x.swap(gate_up_far, 2)
    down_weight_part = dot_rows(inner, grad_all)
    down_part = dot(inner, down_sub).astype(bf16)
    mid_grad_in, down_weight_part, down_part = lax.optimization_barrier(
        (mid_grad_in, down_weight_part, down_part)
    )
    down_own = lax.psum_scatter(down_part, "ctx", scatter_dimension=0, tiled=True)

    mid_scale = own_rows(mlp_scale)
    mid_unit = middle_own * mid_scale
    mid_term = mid_grad_in * gain2
    middle_grad = out_grad[0].astype(f32) + mid_scale * (
        mid_term - mid_unit * jnp.mean(mid_unit * mid_term, axis=-1, keepdims=True)
    )
    mlp_gain_part = jnp.sum(mid_grad_in * mid_unit, axis=0)
    middle_low = middle_grad.astype(bf16)
    att_grad = dot_cols(middle_low, full_out).astype(bf16)
    blocks = cut_columns((att_grad,), 1, None)
    att_grad = lax.all_to_all(blocks, "ctx", 0, 0, tiled=True).reshape(n * rows, -1)
    w_out_part = dot_rows(own_rows(att_low), middle_low)
    down_weight_near, down_weight_far = scatter_seq_near(x, down_weight_part, seq_here)
    att_grad, w_out_part, gate_up_far.value, down_weight_far = lax.optimization_barrier(
        (att_grad, w_out_part, gate_up_far.value, down_weight_far)
    )
    down_weight_far = x.swap(down_weight_far, 2)
    w_out_near, w_out_far = scatter_seq_near(x, w_out_part, seq_here)
    gate_up_sum = (gate_up_near + gate_up_far.value.astype(f32)).astype(bf16)
    w_gate_grad, w_up_grad = to_owners(gate_up_sum, 2, seqs)

    query_acc, key_acc, value_acc = attention_back(
        query, key, value, pos_all, attended, lse, att_grad
    )
    qkv_grad = jnp.concatenate(
        [rotate(query_acc, cosine, -sine), rotate(key_acc, cosine, -sine), value_acc], axis=1
    ).astype(bf16)
    qkv_grad, down_weight_far.value, w_out_far, down_own = lax.optimization_barrier(
        (qkv_grad, down_weight_far.value, w_out_far, down_own)
    )
    hidden_out = (middle_own + down_own.astype(f32)).astype(bf16)
    w_down_grad = down_weight_near + down_weight_far.value.astype(f32)
    w_out_far = x.swap(w_out_far, 2)
    normed_grad_part = dot_cols(qkv_grad, qkv_sub)
    attn_gain_part = jnp.sum(normed_grad_part * (x_all * attn_scale), axis=0)
    beside = jnp.stack([attn_gain_part, mlp_gain_part], axis=1)
    beside = jnp.pad(beside, ((0, 0), (0, 126)))
    qkv_part = jnp.concatenate([dot_rows(normed, qkv_grad), beside], axis=1)
    x_again = Link("seq", 1)
    qkv_near, qkv_far = scatter_seq_near(x_again, qkv_part, seq_here)
    qkv_far, qkv_sum = Box(qkv_far), Box(None)

    def add_far():
        far = x_again.swap(qkv_far, 2)
        qkv_sum.value = (qkv_near + far.value.astype(f32)).astype(bf16)
        return [qkv_sum]

    normed_grad = scatter_halves(
        y, z, normed_grad_part.astype(bf16), here, [lambda: [qkv_far], add_far]
    )
    w_query_grad, w_key_grad, w_value_grad, gain_grads = to_owners(qkv_sum.value, 3, 1, 128)
    gain_grads = gain_grads.astype(f32).reshape(weight_rows, n, 128).sum(axis=1)
    w_out_far, normed_grad = lax.optimization_barrier((w_out_far.value, normed_grad))
    w_out_sum = w_out_near + w_out_far.astype(f32)
    w_out_grad = scatter_ctx_grouped(y, z, w_out_sum, here)

    own_scale = own_rows(attn_scale)
    own_unit = hidden_in[0].astype(f32) * own_scale
    attn_term = normed_grad * gain1
    hidden_grad = middle_grad + own_scale * (
        attn_term - own_unit * jnp.mean(own_unit * attn_term, axis=-1, keepdims=True)
    )
    return (
        hidden_out[None],
        hidden_grad[None],
        gain_grads[:, 0],
        w_query_grad,
        w_key_grad,
        w_value_grad,
        w_out_grad,
        gain_grads[:, 1],
        w_gate_grad,
        w_up_grad,
        w_down_grad,
    )


def solution(mesh):
    tokens = P("seq", "ctx", None)
    whole = P(("seq", "ctx"), None)
    gain = P(("seq", "ctx"))
    local = tuned if mesh.shape["ctx"] == 8 and mesh.shape["seq"] == 4 else plain
    return jax.shard_map(
        local,
        mesh=mesh,
        in_specs=(
            tokens,
            P("seq", "ctx"),
            gain,
            whole,
            whole,
            whole,
            whole,
            gain,
            whole,
            whole,
            whole,
            tokens,
        ),
        out_specs=(tokens, tokens, gain, whole, whole, whole, whole, gain, whole, whole, whole),
        check_vma=False,
    )
```

```python
import math

import jax
import jax.numpy as jnp
from jax import lax
from jax.experimental import pallas as pl
from jax.experimental.pallas import tpu as pltpu
from jax.sharding import PartitionSpec as P

HEADS = 32
HEAD_DIM = 64

eps = 1e-05
rope_base = 130000.0
mask_fill = -1e30
bf16 = jnp.bfloat16
f32 = jnp.float32


def plain_gather_ctx(block):
    return lax.all_gather(block, "ctx", axis=0, tiled=True)


def plain_gather_seq(block):
    return lax.all_gather(block, "seq", axis=0, tiled=True)


def plain_scatter_ctx(total):
    return lax.psum_scatter(total.astype(bf16), "ctx", scatter_dimension=0, tiled=True).astype(f32)


def plain_scatter_seq(total):
    return lax.psum_scatter(total.astype(bf16), "seq", scatter_dimension=0, tiled=True)


def plain_swap_ctx(blocks):
    return lax.all_to_all(blocks, "ctx", 0, 0, tiled=True)


def rms_scale(values):
    return lax.rsqrt(jnp.mean(values * values, axis=-1, keepdims=True) + eps)


def angle_table(positions):
    exponents = jnp.arange(HEAD_DIM // 2, dtype=f32) * (2.0 / HEAD_DIM)
    inverse = jnp.exp(-math.log(rope_base) * exponents)
    return positions.astype(f32)[:, None, None] * inverse[None, None, :]


def rotate(values, cosine, sine_part):
    half_dim = HEAD_DIM // 2
    heads = values.reshape(values.shape[0], -1, HEAD_DIM)
    first_half = heads[..., :half_dim]
    second_half = heads[..., half_dim:]
    return jnp.concatenate(
        [
            first_half * cosine - second_half * sine_part,
            second_half * cosine + first_half * sine_part,
        ],
        axis=-1,
    ).reshape(values.shape)


def dot(left, right):
    return jnp.dot(left, right, preferred_element_type=f32)


def dot_rows(left, right):
    return lax.dot_general(left, right, (((0,), (0,)), ((), ())), preferred_element_type=f32)


def dot_cols(left, right):
    return lax.dot_general(left, right, (((1,), (1,)), ((), ())), preferred_element_type=f32)


def columns_to_owners(weight, groups):
    n = lax.axis_size("ctx")
    rows = weight.shape[0]
    width = weight.shape[1] // (n * groups)
    blocks = weight.reshape(rows, groups, n, width).transpose(2, 0, 1, 3)
    mine = plain_swap_ctx(blocks.reshape(n, rows, groups * width))
    return plain_gather_seq(mine.reshape(n * rows, groups * width))


def columns_from_owners(total, groups):
    n = lax.axis_size("ctx")
    part = plain_scatter_seq(total)
    rows = part.shape[0] // n
    width = part.shape[1] // groups
    back = plain_swap_ctx(part.reshape(n, rows, groups * width))
    back = back.reshape(n, rows, groups, width).transpose(1, 2, 0, 3)
    return back.reshape(rows, groups * n * width)


def attention(query, key, value, positions):
    heads = query.shape[1] // HEAD_DIM
    scale = 1.0 / math.sqrt(HEAD_DIM)
    allowed = positions[None, None, :] <= positions[None, :, None]
    qh, kh, vh = (m.reshape(-1, heads, HEAD_DIM) for m in (query, key, value))
    scores = jnp.einsum("qhd,khd->hqk", qh, kh, preferred_element_type=f32) * scale
    scores = jnp.where(allowed, scores, mask_fill)
    row_max = jnp.max(scores, axis=-1)
    weights = jnp.exp(scores - row_max[:, :, None])
    row_total = jnp.sum(weights, axis=-1)
    mixed = jnp.einsum("hqk,khd->qhd", weights.astype(bf16), vh, preferred_element_type=f32)
    attended = mixed / row_total.T[:, :, None]
    return attended.reshape(query.shape), row_max + jnp.log(row_total)


def attention_back(query, key, value, positions, attended, lse, grad):
    heads = query.shape[1] // HEAD_DIM
    scale = 1.0 / math.sqrt(HEAD_DIM)
    allowed = positions[None, None, :] <= positions[None, :, None]
    qh, kh, vh, gh = (m.reshape(-1, heads, HEAD_DIM) for m in (query, key, value, grad))
    row_delta = jnp.sum(gh.astype(f32) * attended.reshape(-1, heads, HEAD_DIM), axis=-1)
    scores = jnp.einsum("qhd,khd->hqk", qh, kh, preferred_element_type=f32) * scale
    prob = jnp.where(allowed, jnp.exp(scores - lse[:, :, None]), 0.0)
    prob_grad = jnp.einsum("qhd,khd->hqk", gh, vh, preferred_element_type=f32)
    score_grad = (prob * (prob_grad - row_delta.T[:, :, None])).astype(bf16)
    prob_low = prob.astype(bf16)
    value_acc = jnp.einsum("hqk,qhd->khd", prob_low, gh, preferred_element_type=f32)
    query_acc = jnp.einsum("hqk,khd->qhd", score_grad, kh, preferred_element_type=f32) * scale
    key_acc = jnp.einsum("hqk,qhd->khd", score_grad, qh, preferred_element_type=f32) * scale
    return tuple(m.reshape(query.shape) for m in (query_acc, key_acc, value_acc))


def plain(
    hidden_in,
    positions,
    attn_gain,
    w_query,
    w_key,
    w_value,
    w_out,
    mlp_gain,
    w_gate,
    w_up,
    w_down,
    out_grad,
):
    n = lax.axis_size("ctx")
    seqs = lax.axis_size("seq")
    here = lax.axis_index("ctx")
    rows = hidden_in.shape[1]

    def own_rows(whole):
        return lax.dynamic_slice_in_dim(whole, here * rows, rows, 0)

    qkv_sub = columns_to_owners(jnp.concatenate([w_query, w_key, w_value], axis=1), 3)
    x_low = plain_gather_ctx(hidden_in[0])
    pos_all = plain_gather_ctx(positions[0])
    gains = lax.all_gather(jnp.stack([attn_gain, mlp_gain]), ("seq", "ctx"), axis=1, tiled=True)
    full_out = lax.all_gather(w_out, ("seq", "ctx"), axis=0, tiled=True)
    gate_up = columns_to_owners(jnp.concatenate([w_gate, w_up], axis=1), 2 * seqs)
    down_sub = plain_gather_seq(w_down)
    grad_all = plain_gather_ctx(out_grad[0])

    x = x_low.astype(f32)
    attn_scale = rms_scale(x)
    gain1 = gains[0].astype(f32)
    gain2 = gains[1].astype(f32)
    normed = (x * attn_scale * gain1).astype(bf16)
    angles = angle_table(pos_all)
    cosine, sine = jnp.cos(angles), jnp.sin(angles)
    qkv = dot(normed, qkv_sub)
    width = qkv.shape[1] // 3
    query = rotate(qkv[:, :width], cosine, sine).astype(bf16)
    key = rotate(qkv[:, width : 2 * width], cosine, sine).astype(bf16)
    value = qkv[:, 2 * width :].astype(bf16)
    attended, lse = attention(query, key, value, pos_all)
    att_low = lax.all_gather(attended.astype(bf16), "ctx", axis=1, tiled=True)

    middle = x + dot(att_low, full_out)
    mlp_scale = rms_scale(middle)
    normed_mid = (middle * mlp_scale * gain2).astype(bf16)
    gate_up_act = dot(normed_mid, gate_up)
    units = gate_up.shape[1] // 2
    gate_act, up_act = gate_up_act[:, :units], gate_up_act[:, units:]
    sig = jax.nn.sigmoid(gate_act)
    inner = (gate_act * sig * up_act).astype(bf16)
    middle_own = own_rows(middle)
    hidden_out = (middle_own + plain_scatter_ctx(dot(inner, down_sub))).astype(bf16)

    inner_grad = dot_cols(grad_all, down_sub)
    gate_grad = (inner_grad * up_act * sig * (1.0 + gate_act * (1.0 - sig))).astype(bf16)
    up_grad = (inner_grad * gate_act * sig).astype(bf16)
    gate_up_grad = jnp.concatenate([gate_grad, up_grad], axis=1)
    mid_grad_in = plain_scatter_ctx(dot_cols(gate_up_grad, gate_up))
    w_gate_up_grad = columns_from_owners(dot_rows(normed_mid, gate_up_grad), 2 * seqs).astype(f32)
    hidden_units = w_gate.shape[1]
    w_down_grad = plain_scatter_seq(dot_rows(inner, grad_all)).astype(f32)

    mid_scale = own_rows(mlp_scale)
    mid_unit = middle_own * mid_scale
    mid_term = mid_grad_in * gain2
    middle_grad = out_grad[0].astype(f32) + mid_scale * (
        mid_term - mid_unit * jnp.mean(mid_unit * mid_term, axis=-1, keepdims=True)
    )
    mlp_gain_part = jnp.sum(mid_grad_in * mid_unit, axis=0)
    middle_low = middle_grad.astype(bf16)
    att_grad = dot_cols(middle_low, full_out).astype(bf16)
    att_grad = plain_swap_ctx(att_grad.reshape(rows, n, -1).transpose(1, 0, 2)).reshape(n * rows, -1)
    middle_low_all = plain_gather_ctx(middle_low)
    out_rows = w_out.shape[0]
    att_cols = att_low.reshape(n * rows, seqs, n, out_rows)
    att_sub = lax.dynamic_slice_in_dim(att_cols, here, 1, 2).reshape(n * rows, seqs * out_rows)
    w_out_grad = plain_scatter_seq(dot_rows(att_sub, middle_low_all)).astype(f32)

    query_acc, key_acc, value_acc = attention_back(
        query, key, value, pos_all, attended, lse, att_grad
    )
    qkv_grad = jnp.concatenate(
        [rotate(query_acc, cosine, -sine), rotate(key_acc, cosine, -sine), value_acc], axis=1
    ).astype(bf16)
    normed_grad = plain_scatter_ctx(dot_cols(qkv_grad, qkv_sub))
    own_scale = own_rows(attn_scale)
    own_unit = hidden_in[0].astype(f32) * own_scale
    attn_term = normed_grad * gain1
    hidden_grad = middle_grad + own_scale * (
        attn_term - own_unit * jnp.mean(own_unit * attn_term, axis=-1, keepdims=True)
    )
    attn_gain_part = jnp.sum(normed_grad * own_unit, axis=0)
    w_qkv_grad = columns_from_owners(dot_rows(normed, qkv_grad), 3).astype(f32)
    model_width = x.shape[1]
    gain_grads = lax.psum_scatter(
        jnp.stack([attn_gain_part, mlp_gain_part], axis=1),
        ("seq", "ctx"),
        scatter_dimension=0,
        tiled=True,
    )
    return (
        hidden_out[None],
        hidden_grad[None],
        gain_grads[:, 0],
        w_qkv_grad[:, :model_width],
        w_qkv_grad[:, model_width : 2 * model_width],
        w_qkv_grad[:, 2 * model_width :],
        w_out_grad,
        gain_grads[:, 1],
        w_gate_up_grad[:, :hidden_units],
        w_gate_up_grad[:, hidden_units:],
        w_down_grad,
    )


class Box:
    def __init__(self, value):
        self.value = value


def value_of(block):
    return block.value if isinstance(block, Box) else block


def order(block, *boxes):
    values = lax.optimization_barrier((value_of(block),) + tuple(box.value for box in boxes))
    for box, value in zip(boxes, values[1:]):
        box.value = value
    return values[0]


class Link:
    def __init__(self, axis, depth):
        self.axis = axis
        self.depth = depth
        self.arrived = []

    def swap(self, block, mask):
        n = lax.axis_size(self.axis)
        if len(self.arrived) >= self.depth:
            before = order(block, self.arrived[-self.depth])
            if isinstance(block, Box):
                block.value = before
            block = before
        got = Box(lax.ppermute(value_of(block), self.axis, [(i, i ^ mask) for i in range(n)]))
        self.arrived.append(got)
        return got


def place(pieces, places):
    pieces = [value_of(piece) for piece in pieces]
    rows, width = pieces[0].shape
    count = len(pieces)
    shape = (count * rows, width)

    def kernel(places_ref, *refs):
        parts, whole, sems = refs[:count], refs[count], refs[count + 1]
        copies = []
        for i in range(count):
            there = whole.at[pl.ds(pl.multiple_of(places_ref[i] * rows, rows), rows), :]
            copies.append(pltpu.make_async_copy(parts[i], there, sems.at[i]))
        for copy in copies:
            copy.start()
        for copy in copies:
            copy.wait()

    return pl.pallas_call(
        kernel,
        out_shape=jax.ShapeDtypeStruct(shape, pieces[0].dtype),
        in_specs=[pl.BlockSpec(memory_space=pltpu.SMEM)]
        + [pl.BlockSpec(memory_space=pl.ANY)] * count,
        out_specs=pl.BlockSpec(memory_space=pltpu.VMEM),
        scratch_shapes=[pltpu.SemaphoreType.DMA((count,))],
        compiler_params=pltpu.CompilerParams(vmem_limit_bytes=32 * 1024 * 1024),
        cost_estimate=pl.CostEstimate(flops=0, bytes_accessed=4 * rows * width * count, transcendentals=0),
    )(jnp.stack(places).astype(jnp.int32), *pieces)


def cut_columns(weights, groups, beside, devices=None):
    n = lax.axis_size("ctx")
    rows = weights[0].shape[0]
    width = weights[0].shape[1] // (n * groups)
    arrays = list(weights) + ([] if beside is None else [beside])
    total = len(weights) * groups * width + (0 if beside is None else beside.shape[1])

    def kernel(*refs):
        out = refs[-1]
        for i, device in enumerate(devices or range(n)):
            at = 0
            for weight in refs[: len(weights)]:
                for group in range(groups):
                    start = (group * n + device) * width
                    out[i, :, at : at + width] = weight[:, start : start + width]
                    at += width
            if beside is not None:
                out[i, :, at:] = refs[len(weights)][...]

    vmem = pl.BlockSpec(memory_space=pltpu.VMEM)
    return pl.pallas_call(
        kernel,
        out_shape=jax.ShapeDtypeStruct((n, rows, total), bf16),
        in_specs=[vmem] * len(arrays),
        out_specs=vmem,
        compiler_params=pltpu.CompilerParams(vmem_limit_bytes=32 * 1024 * 1024),
    )(*arrays)


def paste_columns(blocks, count, groups, beside=0):
    n, rows, total = blocks.shape
    width = (total - beside) // (count * groups)
    shapes = [jax.ShapeDtypeStruct((rows, groups * n * width), f32)] * count
    if beside:
        shapes.append(jax.ShapeDtypeStruct((rows, n * beside), f32))

    def kernel(ref, *outs):
        for device in range(n):
            at = 0
            for i in range(count):
                for group in range(groups):
                    start = (group * n + device) * width
                    outs[i][:, start : start + width] = ref[device, :, at : at + width].astype(f32)
                    at += width
            if beside:
                start = device * beside
                outs[count][:, start : start + beside] = ref[device, :, at:].astype(f32)

    vmem = pl.BlockSpec(memory_space=pltpu.VMEM)
    return pl.pallas_call(
        kernel,
        out_shape=shapes,
        in_specs=[vmem],
        out_specs=[vmem] * len(shapes),
        compiler_params=pltpu.CompilerParams(vmem_limit_bytes=32 * 1024 * 1024),
    )(blocks)


def ring():
    n = lax.axis_size("ctx")
    return list(range(0, n, 2)) + list(range(n - 1, 0, -2))


def gather_ring(block):
    return lax.all_gather(block, "ctx", axis=0, tiled=True, axis_index_groups=[ring()])


def scatter_ring(total):
    return lax.psum_scatter(
        total, "ctx", scatter_dimension=0, tiled=True, axis_index_groups=[ring()]
    ).astype(f32)


def rearranged(stack, places, columns=False):
    count = len(places)
    rows, width = stack.shape[0] // count, stack.shape[1]

    def kernel(stack_ref, whole, sems):
        copies = []
        for i, to in enumerate(places):
            if columns:
                there = whole.at[:, pl.ds(to * width, width)]
            else:
                there = whole.at[pl.ds(to * rows, rows), :]
            block = stack_ref.at[pl.ds(i * rows, rows), :]
            copies.append(pltpu.make_async_copy(block, there, sems.at[i]))
        for copy in copies:
            copy.start()
        for copy in copies:
            copy.wait()

    shape = (rows, count * width) if columns else stack.shape
    return pl.pallas_call(
        kernel,
        out_shape=jax.ShapeDtypeStruct(shape, stack.dtype),
        in_specs=[pl.BlockSpec(memory_space=pl.ANY)],
        out_specs=pl.BlockSpec(memory_space=pltpu.VMEM),
        scratch_shapes=[pltpu.SemaphoreType.DMA((count,))],
        compiler_params=pltpu.CompilerParams(vmem_limit_bytes=32 * 1024 * 1024),
    )(stack)


def whole_ring():
    n = lax.axis_size("ctx")
    depth = n // 2
    chips = []
    for far, side, upward in ((0, 0, True), (0, 1, False), (1, 1, True), (1, 0, False)):
        levels = range(depth) if upward else range(depth - 1, -1, -1)
        chips += [(far, 2 * level + side) for level in levels]
    return [(2 * far + core) * n + ctx for far, ctx in chips for core in range(2)]


def core_swap(block):
    n = lax.axis_size("seq")
    return Box(lax.ppermute(value_of(block), "seq", [(i, i ^ 1) for i in range(n)]))


def gather_seq(x, block):
    far = x.swap(block, 2)
    return [(0, block), (1, core_swap(block)), (2, far), (3, core_swap(far))]


def scatter_seq_near(total, here):
    rows = total.shape[0] // 4

    def piece(offset):
        return lax.dynamic_slice_in_dim(total, (here ^ offset) * rows, rows, 0)

    got = core_swap(jnp.concatenate([piece(3), piece(1)], axis=0).astype(bf16))
    return piece(0) + got.value[rows:].astype(f32), (
        piece(2) + got.value[:rows].astype(f32)
    ).astype(bf16)


def to_owners(part, count, groups, beside=0):
    n = lax.axis_size("ctx")
    blocks = lax.all_to_all(part.reshape(n, -1, part.shape[1]), "ctx", 0, 0, tiled=True)
    return paste_columns(blocks, count, groups, beside)


def tuned(
    hidden_in,
    positions,
    attn_gain,
    w_query,
    w_key,
    w_value,
    w_out,
    mlp_gain,
    w_gate,
    w_up,
    w_down,
    out_grad,
):
    n = lax.axis_size("ctx")
    seqs = lax.axis_size("seq")
    here = lax.axis_index("ctx")
    seq_here = lax.axis_index("seq")
    rows = hidden_in.shape[1]
    weight_rows = w_query.shape[0]
    x = Link("seq", 1)
    place_here = jnp.where(here % 2 == 0, here // 2, n - 1 - here // 2)

    def own_rows(whole):
        return lax.dynamic_slice_in_dim(whole, place_here * rows, rows, 0)

    def from_devices(held):
        return place([part for _, part in held], [seq_here ^ o for o, _ in held])

    own_pos = positions[0].reshape(weight_rows, -1)
    per_row = own_pos.shape[1]
    beside = jnp.concatenate(
        [
            attn_gain[:, None],
            mlp_gain[:, None],
            (own_pos // 64).astype(bf16),
            (own_pos % 64).astype(bf16),
        ],
        axis=1,
    )
    beside = jnp.pad(beside, ((0, 0), (0, 128 - beside.shape[1])))
    x_low = gather_ring(hidden_in[0])
    down_steps = gather_seq(Link("seq", 1), w_down)
    blocks = cut_columns((w_query, w_key, w_value), 1, beside)
    qkv_mine = lax.all_to_all(blocks, "ctx", 0, 0, tiled=True).reshape(n * weight_rows, -1)
    down_far = down_steps[2][1]
    late_out, qkv_mine, down_far.value = lax.optimization_barrier((w_out, qkv_mine, down_far.value))
    qkv_steps = gather_seq(x, qkv_mine)
    far = qkv_steps[2][1]
    late_gate, late_up, far.value = lax.optimization_barrier((w_gate, w_up, far.value))
    out_stack = lax.all_gather(
        late_out, ("seq", "ctx"), axis=0, tiled=True, axis_index_groups=[whole_ring()]
    )
    blocks = cut_columns((late_gate, late_up), seqs, None)
    gate_up = lax.all_to_all(blocks, "ctx", 0, 0, tiled=True).reshape(n * weight_rows, -1)
    qkv_sub = from_devices(qkv_steps)
    down_sub = from_devices(down_steps)
    pos_cuts = qkv_mine[:, -128:].astype(jnp.int32)
    pos_all = pos_cuts[:, 2 : 2 + per_row] * 64 + pos_cuts[:, 2 + per_row : 2 + 2 * per_row]
    pos_all = pos_all.reshape(n, rows)
    pos_all = jnp.concatenate([pos_all[device] for device in ring()])
    gain1 = qkv_sub[:, -128].astype(f32)
    gain2 = qkv_sub[:, -127].astype(f32)
    qkv_sub = qkv_sub[:, :-128]

    x_all = x_low.astype(f32)
    attn_scale = rms_scale(x_all)
    normed = (x_all * attn_scale * gain1).astype(bf16)
    angles = angle_table(pos_all)
    cosine, sine = jnp.cos(angles), jnp.sin(angles)
    qkv = dot(normed, qkv_sub)
    width = qkv.shape[1] // 3
    query = rotate(qkv[:, :width], cosine, sine).astype(bf16)
    key = rotate(qkv[:, width : 2 * width], cosine, sine).astype(bf16)
    value = qkv[:, 2 * width :].astype(bf16)
    split = width // 2
    halves = [slice(0, split), slice(split, width)]
    att_first, lse_first = attention(*(m[:, halves[0]] for m in (query, key, value)), pos_all)
    att_second, lse_second = attention(*(m[:, halves[1]] for m in (query, key, value)), pos_all)
    att_low = jnp.concatenate([att_first, att_second], axis=1).astype(bf16)
    att_low, out_stack, gate_up = lax.optimization_barrier((att_low, out_stack, gate_up))
    gate_up = from_devices(gather_seq(x, gate_up))
    att_stack = gather_ring(att_low)
    full_out = rearranged(out_stack, whole_ring())
    att_low = rearranged(att_stack, ring(), columns=True)
    late_grad, att_low = lax.optimization_barrier((out_grad[0], att_low))
    grad_all = gather_ring(late_grad)

    middle = x_all + dot(att_low, full_out)
    mlp_scale = rms_scale(middle)
    normed_mid = (middle * mlp_scale * gain2).astype(bf16)
    gate_up_act = dot(normed_mid, gate_up)
    units = gate_up.shape[1] // 2
    gate_act, up_act = gate_up_act[:, :units], gate_up_act[:, units:]
    sig = jax.nn.sigmoid(gate_act)
    inner = (gate_act * sig * up_act).astype(bf16)
    middle_own = own_rows(middle)

    inner_grad = lax.optimization_barrier(dot_cols(grad_all, down_sub))
    gate_grad = (inner_grad * up_act * sig * (1.0 + gate_act * (1.0 - sig))).astype(bf16)
    up_grad = (inner_grad * gate_act * sig).astype(bf16)
    gate_up_grad = lax.optimization_barrier(jnp.concatenate([gate_grad, up_grad], axis=1))
    mid_grad_part = dot_cols(gate_up_grad, gate_up).astype(bf16)
    gate_up_near, gate_up_far = scatter_seq_near(dot_rows(normed_mid, gate_up_grad), seq_here)
    mid_grad_in = scatter_ring(mid_grad_part)
    down_weight_part = dot_rows(inner, grad_all)
    down_part = dot(inner, down_sub).astype(bf16)
    mid_grad_in, down_weight_part, down_part, gate_up_far = lax.optimization_barrier(
        (mid_grad_in, down_weight_part, down_part, gate_up_far)
    )
    gate_up_far = x.swap(gate_up_far, 2)
    down_own = scatter_ring(down_part)

    mid_scale = own_rows(mlp_scale)
    mid_unit = middle_own * mid_scale
    mid_term = mid_grad_in * gain2
    middle_grad = out_grad[0].astype(f32) + mid_scale * (
        mid_term - mid_unit * jnp.mean(mid_unit * mid_term, axis=-1, keepdims=True)
    )
    mlp_gain_part = jnp.sum(mid_grad_in * mid_unit, axis=0)
    middle_low = middle_grad.astype(bf16)
    att_grad = dot_cols(middle_low, full_out).astype(bf16)
    blocks = cut_columns((att_grad,), 1, None, ring())
    att_grad = lax.all_to_all(blocks, "ctx", 0, 0, tiled=True, axis_index_groups=[ring()])
    att_grad = att_grad.reshape(n * rows, -1)
    middle_low_all = gather_ring(middle_low)
    gate_up_sum = (gate_up_near + gate_up_far.value.astype(f32)).astype(bf16)
    att_grad, gate_up_sum, down_own = lax.optimization_barrier((att_grad, gate_up_sum, down_own))
    w_gate_up = lax.all_to_all(gate_up_sum.reshape(n, weight_rows, -1), "ctx", 0, 0, tiled=True)

    grads = [
        attention_back(
            *(m[:, halves[0]] for m in (query, key, value)), pos_all, att_first, lse_first, att_grad[:, halves[0]]
        )
    ]
    down_weight_near, down_weight_far = scatter_seq_near(down_weight_part, seq_here)
    att_grad, down_weight_far, grads[0] = lax.optimization_barrier(
        (att_grad, down_weight_far, grads[0])
    )
    down_weight_far = x.swap(down_weight_far, 2)
    grads.append(
        attention_back(
            *(m[:, halves[1]] for m in (query, key, value)), pos_all, att_second, lse_second, att_grad[:, halves[1]]
        )
    )
    query_acc, key_acc, value_acc = (jnp.concatenate(pair, axis=1) for pair in zip(*grads))
    qkv_grad = jnp.concatenate(
        [rotate(query_acc, cosine, -sine), rotate(key_acc, cosine, -sine), value_acc], axis=1
    ).astype(bf16)
    out_rows = w_out.shape[0]
    att_sub = jnp.concatenate(
        [
            lax.dynamic_slice_in_dim(att_low, (i * n + here) * out_rows, out_rows, 1)
            for i in range(seqs)
        ],
        axis=1,
    )
    w_out_near, w_out_far = scatter_seq_near(dot_rows(att_sub, middle_low_all), seq_here)
    hidden_out = (middle_own + down_own).astype(bf16)
    qkv_grad, w_gate_up, down_weight_far.value = lax.optimization_barrier(
        (qkv_grad, w_gate_up, down_weight_far.value)
    )
    normed_grad_part = dot_cols(qkv_grad, qkv_sub)
    attn_gain_part = jnp.sum(normed_grad_part * (x_all * attn_scale), axis=0)
    beside = jnp.stack([attn_gain_part, mlp_gain_part], axis=1)
    beside = jnp.pad(beside, ((0, 0), (0, 126)))
    qkv_part = jnp.concatenate([dot_rows(normed, qkv_grad), beside], axis=1)
    qkv_near, qkv_far = scatter_seq_near(qkv_part, seq_here)
    normed_grad = scatter_ring(normed_grad_part.astype(bf16))
    qkv_far = Link("seq", 1).swap(qkv_far, 2)
    qkv_sum = (qkv_near + qkv_far.value.astype(f32)).astype(bf16)
    w_query_grad, w_key_grad, w_value_grad, gain_grads = to_owners(qkv_sum, 3, 1, 128)
    gain_grads = gain_grads.astype(f32).reshape(weight_rows, n, 128).sum(axis=1)
    w_out_grad = w_out_near + Link("seq", 1).swap(w_out_far, 2).value.astype(f32)
    down_weight_far, w_gate_up, normed_grad = lax.optimization_barrier(
        (down_weight_far.value, w_gate_up, normed_grad)
    )
    w_gate_grad, w_up_grad = paste_columns(w_gate_up, 2, seqs)
    w_down_grad = down_weight_near + down_weight_far.astype(f32)

    own_scale = own_rows(attn_scale)
    own_unit = hidden_in[0].astype(f32) * own_scale
    attn_term = normed_grad * gain1
    hidden_grad = middle_grad + own_scale * (
        attn_term - own_unit * jnp.mean(own_unit * attn_term, axis=-1, keepdims=True)
    )
    return (
        hidden_out[None],
        hidden_grad[None],
        gain_grads[:, 0],
        w_query_grad,
        w_key_grad,
        w_value_grad,
        w_out_grad,
        gain_grads[:, 1],
        w_gate_grad,
        w_up_grad,
        w_down_grad,
    )


def solution(mesh):
    tokens = P("seq", "ctx", None)
    whole = P(("seq", "ctx"), None)
    gain = P(("seq", "ctx"))
    local = tuned if mesh.shape["ctx"] == 8 and mesh.shape["seq"] == 4 else plain
    return jax.shard_map(
        local,
        mesh=mesh,
        in_specs=(
            tokens,
            P("seq", "ctx"),
            gain,
            whole,
            whole,
            whole,
            whole,
            gain,
            whole,
            whole,
            whole,
            tokens,
        ),
        out_specs=(tokens, tokens, gain, whole, whole, whole, whole, gain, whole, whole, whole),
        check_vma=False,
    )
```

```python
import math

import jax
import jax.numpy as jnp
from jax import lax
from jax.experimental import pallas as pl
from jax.experimental.pallas import tpu as pltpu
from jax.sharding import PartitionSpec as P

HEADS = 32
HEAD_DIM = 64

eps = 1e-05
rope_base = 130000.0
mask_fill = -1e30
bf16 = jnp.bfloat16
f32 = jnp.float32


def plain_gather_ctx(block):
    return lax.all_gather(block, "ctx", axis=0, tiled=True)


def plain_gather_seq(block):
    return lax.all_gather(block, "seq", axis=0, tiled=True)


def plain_scatter_ctx(total):
    return lax.psum_scatter(total.astype(bf16), "ctx", scatter_dimension=0, tiled=True).astype(f32)


def plain_scatter_seq(total):
    return lax.psum_scatter(total.astype(bf16), "seq", scatter_dimension=0, tiled=True)


def plain_swap_ctx(blocks):
    return lax.all_to_all(blocks, "ctx", 0, 0, tiled=True)


def rms_scale(values):
    return lax.rsqrt(jnp.mean(values * values, axis=-1, keepdims=True) + eps)


def angle_table(positions):
    exponents = jnp.arange(HEAD_DIM // 2, dtype=f32) * (2.0 / HEAD_DIM)
    inverse = jnp.exp(-math.log(rope_base) * exponents)
    return positions.astype(f32)[:, None, None] * inverse[None, None, :]


def rotate(values, cosine, sine_part):
    half_dim = HEAD_DIM // 2
    heads = values.reshape(values.shape[0], -1, HEAD_DIM)
    first_half = heads[..., :half_dim]
    second_half = heads[..., half_dim:]
    return jnp.concatenate(
        [
            first_half * cosine - second_half * sine_part,
            second_half * cosine + first_half * sine_part,
        ],
        axis=-1,
    ).reshape(values.shape)


def dot(left, right):
    return jnp.dot(left, right, preferred_element_type=f32)


def dot_rows(left, right):
    return lax.dot_general(left, right, (((0,), (0,)), ((), ())), preferred_element_type=f32)


def dot_cols(left, right):
    return lax.dot_general(left, right, (((1,), (1,)), ((), ())), preferred_element_type=f32)


def columns_to_owners(weight, groups):
    n = lax.axis_size("ctx")
    rows = weight.shape[0]
    width = weight.shape[1] // (n * groups)
    blocks = weight.reshape(rows, groups, n, width).transpose(2, 0, 1, 3)
    mine = plain_swap_ctx(blocks.reshape(n, rows, groups * width))
    return plain_gather_seq(mine.reshape(n * rows, groups * width))


def columns_from_owners(total, groups):
    n = lax.axis_size("ctx")
    part = plain_scatter_seq(total)
    rows = part.shape[0] // n
    width = part.shape[1] // groups
    back = plain_swap_ctx(part.reshape(n, rows, groups * width))
    back = back.reshape(n, rows, groups, width).transpose(1, 2, 0, 3)
    return back.reshape(rows, groups * n * width)


def attention(query, key, value, positions):
    heads = query.shape[1] // HEAD_DIM
    scale = 1.0 / math.sqrt(HEAD_DIM)
    allowed = positions[None, None, :] <= positions[None, :, None]
    qh, kh, vh = (m.reshape(-1, heads, HEAD_DIM) for m in (query, key, value))
    scores = jnp.einsum("qhd,khd->hqk", qh, kh, preferred_element_type=f32) * scale
    scores = jnp.where(allowed, scores, mask_fill)
    row_max = jnp.max(scores, axis=-1)
    weights = jnp.exp(scores - row_max[:, :, None])
    row_total = jnp.sum(weights, axis=-1)
    mixed = jnp.einsum("hqk,khd->qhd", weights.astype(bf16), vh, preferred_element_type=f32)
    attended = mixed / row_total.T[:, :, None]
    return attended.reshape(query.shape), row_max + jnp.log(row_total)


def attention_back(query, key, value, positions, attended, lse, grad):
    heads = query.shape[1] // HEAD_DIM
    scale = 1.0 / math.sqrt(HEAD_DIM)
    allowed = positions[None, None, :] <= positions[None, :, None]
    qh, kh, vh, gh = (m.reshape(-1, heads, HEAD_DIM) for m in (query, key, value, grad))
    row_delta = jnp.sum(gh.astype(f32) * attended.reshape(-1, heads, HEAD_DIM), axis=-1)
    scores = jnp.einsum("qhd,khd->hqk", qh, kh, preferred_element_type=f32) * scale
    prob = jnp.where(allowed, jnp.exp(scores - lse[:, :, None]), 0.0)
    prob_grad = jnp.einsum("qhd,khd->hqk", gh, vh, preferred_element_type=f32)
    score_grad = (prob * (prob_grad - row_delta.T[:, :, None])).astype(bf16)
    prob_low = prob.astype(bf16)
    value_acc = jnp.einsum("hqk,qhd->khd", prob_low, gh, preferred_element_type=f32)
    query_acc = jnp.einsum("hqk,khd->qhd", score_grad, kh, preferred_element_type=f32) * scale
    key_acc = jnp.einsum("hqk,qhd->khd", score_grad, qh, preferred_element_type=f32) * scale
    return tuple(m.reshape(query.shape) for m in (query_acc, key_acc, value_acc))


def plain(
    hidden_in,
    positions,
    attn_gain,
    w_query,
    w_key,
    w_value,
    w_out,
    mlp_gain,
    w_gate,
    w_up,
    w_down,
    out_grad,
):
    n = lax.axis_size("ctx")
    seqs = lax.axis_size("seq")
    here = lax.axis_index("ctx")
    rows = hidden_in.shape[1]

    def own_rows(whole):
        return lax.dynamic_slice_in_dim(whole, here * rows, rows, 0)

    qkv_sub = columns_to_owners(jnp.concatenate([w_query, w_key, w_value], axis=1), 3)
    x_low = plain_gather_ctx(hidden_in[0])
    pos_all = plain_gather_ctx(positions[0])
    gains = lax.all_gather(jnp.stack([attn_gain, mlp_gain]), ("seq", "ctx"), axis=1, tiled=True)
    full_out = lax.all_gather(w_out, ("seq", "ctx"), axis=0, tiled=True)
    gate_up = columns_to_owners(jnp.concatenate([w_gate, w_up], axis=1), 2 * seqs)
    down_sub = plain_gather_seq(w_down)
    grad_all = plain_gather_ctx(out_grad[0])

    x = x_low.astype(f32)
    attn_scale = rms_scale(x)
    gain1 = gains[0].astype(f32)
    gain2 = gains[1].astype(f32)
    normed = (x * attn_scale * gain1).astype(bf16)
    angles = angle_table(pos_all)
    cosine, sine = jnp.cos(angles), jnp.sin(angles)
    qkv = dot(normed, qkv_sub)
    width = qkv.shape[1] // 3
    query = rotate(qkv[:, :width], cosine, sine).astype(bf16)
    key = rotate(qkv[:, width : 2 * width], cosine, sine).astype(bf16)
    value = qkv[:, 2 * width :].astype(bf16)
    attended, lse = attention(query, key, value, pos_all)
    att_low = lax.all_gather(attended.astype(bf16), "ctx", axis=1, tiled=True)

    middle = x + dot(att_low, full_out)
    mlp_scale = rms_scale(middle)
    normed_mid = (middle * mlp_scale * gain2).astype(bf16)
    gate_up_act = dot(normed_mid, gate_up)
    units = gate_up.shape[1] // 2
    gate_act, up_act = gate_up_act[:, :units], gate_up_act[:, units:]
    sig = jax.nn.sigmoid(gate_act)
    inner = (gate_act * sig * up_act).astype(bf16)
    middle_own = own_rows(middle)
    hidden_out = (middle_own + plain_scatter_ctx(dot(inner, down_sub))).astype(bf16)

    inner_grad = dot_cols(grad_all, down_sub)
    gate_grad = (inner_grad * up_act * sig * (1.0 + gate_act * (1.0 - sig))).astype(bf16)
    up_grad = (inner_grad * gate_act * sig).astype(bf16)
    gate_up_grad = jnp.concatenate([gate_grad, up_grad], axis=1)
    mid_grad_in = plain_scatter_ctx(dot_cols(gate_up_grad, gate_up))
    w_gate_up_grad = columns_from_owners(dot_rows(normed_mid, gate_up_grad), 2 * seqs).astype(f32)
    hidden_units = w_gate.shape[1]
    w_down_grad = plain_scatter_seq(dot_rows(inner, grad_all)).astype(f32)

    mid_scale = own_rows(mlp_scale)
    mid_unit = middle_own * mid_scale
    mid_term = mid_grad_in * gain2
    middle_grad = out_grad[0].astype(f32) + mid_scale * (
        mid_term - mid_unit * jnp.mean(mid_unit * mid_term, axis=-1, keepdims=True)
    )
    mlp_gain_part = jnp.sum(mid_grad_in * mid_unit, axis=0)
    middle_low = middle_grad.astype(bf16)
    att_grad = dot_cols(middle_low, full_out).astype(bf16)
    att_grad = plain_swap_ctx(att_grad.reshape(rows, n, -1).transpose(1, 0, 2)).reshape(n * rows, -1)
    middle_low_all = plain_gather_ctx(middle_low)
    out_rows = w_out.shape[0]
    att_cols = att_low.reshape(n * rows, seqs, n, out_rows)
    att_sub = lax.dynamic_slice_in_dim(att_cols, here, 1, 2).reshape(n * rows, seqs * out_rows)
    w_out_grad = plain_scatter_seq(dot_rows(att_sub, middle_low_all)).astype(f32)

    query_acc, key_acc, value_acc = attention_back(
        query, key, value, pos_all, attended, lse, att_grad
    )
    qkv_grad = jnp.concatenate(
        [rotate(query_acc, cosine, -sine), rotate(key_acc, cosine, -sine), value_acc], axis=1
    ).astype(bf16)
    normed_grad = plain_scatter_ctx(dot_cols(qkv_grad, qkv_sub))
    own_scale = own_rows(attn_scale)
    own_unit = hidden_in[0].astype(f32) * own_scale
    attn_term = normed_grad * gain1
    hidden_grad = middle_grad + own_scale * (
        attn_term - own_unit * jnp.mean(own_unit * attn_term, axis=-1, keepdims=True)
    )
    attn_gain_part = jnp.sum(normed_grad * own_unit, axis=0)
    w_qkv_grad = columns_from_owners(dot_rows(normed, qkv_grad), 3).astype(f32)
    model_width = x.shape[1]
    gain_grads = lax.psum_scatter(
        jnp.stack([attn_gain_part, mlp_gain_part], axis=1),
        ("seq", "ctx"),
        scatter_dimension=0,
        tiled=True,
    )
    return (
        hidden_out[None],
        hidden_grad[None],
        gain_grads[:, 0],
        w_qkv_grad[:, :model_width],
        w_qkv_grad[:, model_width : 2 * model_width],
        w_qkv_grad[:, 2 * model_width :],
        w_out_grad,
        gain_grads[:, 1],
        w_gate_up_grad[:, :hidden_units],
        w_gate_up_grad[:, hidden_units:],
        w_down_grad,
    )


class Box:
    def __init__(self, value):
        self.value = value


def value_of(block):
    return block.value if isinstance(block, Box) else block


def order(block, *boxes):
    values = lax.optimization_barrier((value_of(block),) + tuple(box.value for box in boxes))
    for box, value in zip(boxes, values[1:]):
        box.value = value
    return values[0]


class Link:
    def __init__(self, axis, depth):
        self.axis = axis
        self.depth = depth
        self.arrived = []

    def swap(self, block, mask):
        n = lax.axis_size(self.axis)
        if len(self.arrived) >= self.depth:
            before = order(block, self.arrived[-self.depth])
            if isinstance(block, Box):
                block.value = before
            block = before
        got = Box(lax.ppermute(value_of(block), self.axis, [(i, i ^ mask) for i in range(n)]))
        self.arrived.append(got)
        return got


def place(pieces, places):
    pieces = [value_of(piece) for piece in pieces]
    rows, width = pieces[0].shape
    count = len(pieces)
    shape = (count * rows, width)

    def kernel(places_ref, *refs):
        parts, whole, sems = refs[:count], refs[count], refs[count + 1]
        copies = []
        for i in range(count):
            there = whole.at[pl.ds(pl.multiple_of(places_ref[i] * rows, rows), rows), :]
            copies.append(pltpu.make_async_copy(parts[i], there, sems.at[i]))
        for copy in copies:
            copy.start()
        for copy in copies:
            copy.wait()

    return pl.pallas_call(
        kernel,
        out_shape=jax.ShapeDtypeStruct(shape, pieces[0].dtype),
        in_specs=[pl.BlockSpec(memory_space=pltpu.SMEM)]
        + [pl.BlockSpec(memory_space=pl.ANY)] * count,
        out_specs=pl.BlockSpec(memory_space=pltpu.VMEM),
        scratch_shapes=[pltpu.SemaphoreType.DMA((count,))],
        compiler_params=pltpu.CompilerParams(vmem_limit_bytes=32 * 1024 * 1024),
        cost_estimate=pl.CostEstimate(flops=0, bytes_accessed=4 * rows * width * count, transcendentals=0),
    )(jnp.stack(places).astype(jnp.int32), *pieces)


def cut_columns(weights, groups, beside, devices=None):
    n = lax.axis_size("ctx")
    rows = weights[0].shape[0]
    width = weights[0].shape[1] // (n * groups)
    arrays = list(weights) + ([] if beside is None else [beside])
    total = len(weights) * groups * width + (0 if beside is None else beside.shape[1])

    def kernel(*refs):
        out = refs[-1]
        for i, device in enumerate(devices or range(n)):
            at = 0
            for weight in refs[: len(weights)]:
                for group in range(groups):
                    start = (group * n + device) * width
                    out[i, :, at : at + width] = weight[:, start : start + width]
                    at += width
            if beside is not None:
                out[i, :, at:] = refs[len(weights)][...]

    vmem = pl.BlockSpec(memory_space=pltpu.VMEM)
    return pl.pallas_call(
        kernel,
        out_shape=jax.ShapeDtypeStruct((n, rows, total), bf16),
        in_specs=[vmem] * len(arrays),
        out_specs=vmem,
        compiler_params=pltpu.CompilerParams(vmem_limit_bytes=32 * 1024 * 1024),
    )(*arrays)


def paste_columns(blocks, count, groups, beside=0):
    n, rows, total = blocks.shape
    width = (total - beside) // (count * groups)
    shapes = [jax.ShapeDtypeStruct((rows, groups * n * width), f32)] * count
    if beside:
        shapes.append(jax.ShapeDtypeStruct((rows, n * beside), f32))

    def kernel(ref, *outs):
        for device in range(n):
            at = 0
            for i in range(count):
                for group in range(groups):
                    start = (group * n + device) * width
                    outs[i][:, start : start + width] = ref[device, :, at : at + width].astype(f32)
                    at += width
            if beside:
                start = device * beside
                outs[count][:, start : start + beside] = ref[device, :, at:].astype(f32)

    vmem = pl.BlockSpec(memory_space=pltpu.VMEM)
    return pl.pallas_call(
        kernel,
        out_shape=shapes,
        in_specs=[vmem],
        out_specs=[vmem] * len(shapes),
        compiler_params=pltpu.CompilerParams(vmem_limit_bytes=32 * 1024 * 1024),
    )(blocks)


def ring():
    n = lax.axis_size("ctx")
    return list(range(0, n, 2)) + list(range(n - 1, 0, -2))


def gather_ring(block):
    return lax.all_gather(block, "ctx", axis=0, tiled=True, axis_index_groups=[ring()])


def scatter_ring(total):
    return lax.psum_scatter(
        total, "ctx", scatter_dimension=0, tiled=True, axis_index_groups=[ring()]
    ).astype(f32)


def rearranged(stack, places, columns=False):
    count = len(places)
    rows, width = stack.shape[0] // count, stack.shape[1]

    def kernel(stack_ref, whole, sems):
        copies = []
        for i, to in enumerate(places):
            if columns:
                there = whole.at[:, pl.ds(to * width, width)]
            else:
                there = whole.at[pl.ds(to * rows, rows), :]
            block = stack_ref.at[pl.ds(i * rows, rows), :]
            copies.append(pltpu.make_async_copy(block, there, sems.at[i]))
        for copy in copies:
            copy.start()
        for copy in copies:
            copy.wait()

    shape = (rows, count * width) if columns else stack.shape
    return pl.pallas_call(
        kernel,
        out_shape=jax.ShapeDtypeStruct(shape, stack.dtype),
        in_specs=[pl.BlockSpec(memory_space=pl.ANY)],
        out_specs=pl.BlockSpec(memory_space=pltpu.VMEM),
        scratch_shapes=[pltpu.SemaphoreType.DMA((count,))],
        compiler_params=pltpu.CompilerParams(vmem_limit_bytes=32 * 1024 * 1024),
    )(stack)


def whole_ring():
    n = lax.axis_size("ctx")
    depth = n // 2
    chips = []
    for far, side, upward in ((0, 0, True), (0, 1, False), (1, 1, True), (1, 0, False)):
        levels = range(depth) if upward else range(depth - 1, -1, -1)
        chips += [(far, 2 * level + side) for level in levels]
    return [(2 * far + core) * n + ctx for far, ctx in chips for core in range(2)]


def core_swap(block):
    n = lax.axis_size("seq")
    return Box(lax.ppermute(value_of(block), "seq", [(i, i ^ 1) for i in range(n)]))


def gather_seq(x, block):
    far = x.swap(block, 2)
    return [(0, block), (1, core_swap(block)), (2, far), (3, core_swap(far))]


def scatter_seq_near(total, here):
    rows = total.shape[0] // 4

    def piece(offset):
        return lax.dynamic_slice_in_dim(total, (here ^ offset) * rows, rows, 0)

    got = core_swap(jnp.concatenate([piece(3), piece(1)], axis=0).astype(bf16))
    return piece(0) + got.value[rows:].astype(f32), (
        piece(2) + got.value[:rows].astype(f32)
    ).astype(bf16)


def to_owners(part, count, groups, beside=0):
    n = lax.axis_size("ctx")
    blocks = lax.all_to_all(part.reshape(n, -1, part.shape[1]), "ctx", 0, 0, tiled=True)
    return paste_columns(blocks, count, groups, beside)


def tuned(
    hidden_in,
    positions,
    attn_gain,
    w_query,
    w_key,
    w_value,
    w_out,
    mlp_gain,
    w_gate,
    w_up,
    w_down,
    out_grad,
):
    n = lax.axis_size("ctx")
    seqs = lax.axis_size("seq")
    here = lax.axis_index("ctx")
    seq_here = lax.axis_index("seq")
    rows = hidden_in.shape[1]
    weight_rows = w_query.shape[0]
    x = Link("seq", 1)
    place_here = jnp.where(here % 2 == 0, here // 2, n - 1 - here // 2)

    def own_rows(whole):
        return lax.dynamic_slice_in_dim(whole, place_here * rows, rows, 0)

    def from_devices(held):
        return place([part for _, part in held], [seq_here ^ o for o, _ in held])

    own_pos = positions[0].reshape(weight_rows, -1)
    per_row = own_pos.shape[1]
    beside = jnp.concatenate(
        [
            attn_gain[:, None],
            mlp_gain[:, None],
            (own_pos // 64).astype(bf16),
            (own_pos % 64).astype(bf16),
        ],
        axis=1,
    )
    beside = jnp.pad(beside, ((0, 0), (0, 128 - beside.shape[1])))
    x_low = gather_ring(hidden_in[0])
    down_steps = gather_seq(Link("seq", 1), w_down)
    blocks = cut_columns((w_query, w_key, w_value), 1, beside)
    qkv_mine = lax.all_to_all(blocks, "ctx", 0, 0, tiled=True).reshape(n * weight_rows, -1)
    down_far = down_steps[2][1]
    late_out, late_gate, late_up, qkv_mine, down_far.value = lax.optimization_barrier(
        (w_out, w_gate, w_up, qkv_mine, down_far.value)
    )
    qkv_steps = gather_seq(x, qkv_mine)
    out_stack = lax.all_gather(
        late_out, ("seq", "ctx"), axis=0, tiled=True, axis_index_groups=[whole_ring()]
    )
    blocks = cut_columns((late_gate, late_up), seqs, None)
    gate_up = lax.all_to_all(blocks, "ctx", 0, 0, tiled=True).reshape(n * weight_rows, -1)
    qkv_sub = from_devices(qkv_steps)
    down_sub = from_devices(down_steps)
    pos_cuts = qkv_mine[:, -128:].astype(jnp.int32)
    pos_all = pos_cuts[:, 2 : 2 + per_row] * 64 + pos_cuts[:, 2 + per_row : 2 + 2 * per_row]
    pos_all = pos_all.reshape(n, rows)
    pos_all = jnp.concatenate([pos_all[device] for device in ring()])
    gain1 = qkv_sub[:, -128].astype(f32)
    gain2 = qkv_sub[:, -127].astype(f32)
    qkv_sub = qkv_sub[:, :-128]

    x_all = x_low.astype(f32)
    attn_scale = rms_scale(x_all)
    normed = (x_all * attn_scale * gain1).astype(bf16)
    angles = angle_table(pos_all)
    cosine, sine = jnp.cos(angles), jnp.sin(angles)
    qkv = dot(normed, qkv_sub)
    width = qkv.shape[1] // 3
    query = rotate(qkv[:, :width], cosine, sine).astype(bf16)
    key = rotate(qkv[:, width : 2 * width], cosine, sine).astype(bf16)
    value = qkv[:, 2 * width :].astype(bf16)
    split = width // 2
    halves = [slice(0, split), slice(split, width)]
    att_first, lse_first = attention(*(m[:, halves[0]] for m in (query, key, value)), pos_all)
    value, gate_up = lax.optimization_barrier((value, gate_up))
    att_second, lse_second = attention(*(m[:, halves[1]] for m in (query, key, value)), pos_all)
    att_low = jnp.concatenate([att_first, att_second], axis=1).astype(bf16)
    cut = gate_up.shape[0] // 2
    parts = [gate_up[:cut], gate_up[cut:]]
    far = [x.swap(parts[0], 2)]
    att_low, out_stack, far[0].value = lax.optimization_barrier((att_low, out_stack, far[0].value))
    att_stack = gather_ring(att_low)
    far.append(x.swap(parts[1], 2))
    held = []
    for part, other in zip(parts, far):
        held += [(0, part), (1, core_swap(part)), (2, other), (3, core_swap(other))]
    gate_up = place(
        [part for _, part in held],
        [(seq_here ^ o) * 2 + i // 4 for i, (o, _) in enumerate(held)],
    )
    full_out = rearranged(out_stack, whole_ring())
    late_grad, att_stack, full_out, gate_up, down_sub = lax.optimization_barrier(
        (out_grad[0], att_stack, full_out, gate_up, down_sub)
    )
    grad_all = gather_ring(late_grad)
    att_low = rearranged(att_stack, ring(), columns=True)

    middle = x_all + dot(att_low, full_out)
    mlp_scale = rms_scale(middle)
    normed_mid = (middle * mlp_scale * gain2).astype(bf16)
    gate_up_act = dot(normed_mid, gate_up)
    units = gate_up.shape[1] // 2
    gate_act, up_act = gate_up_act[:, :units], gate_up_act[:, units:]
    sig = jax.nn.sigmoid(gate_act)
    inner = (gate_act * sig * up_act).astype(bf16)
    middle_own = own_rows(middle)

    down_part = dot(inner, down_sub).astype(bf16)
    grad_all, down_part = lax.optimization_barrier((grad_all, down_part))
    down_own = scatter_ring(down_part)
    inner_grad = lax.optimization_barrier(dot_cols(grad_all, down_sub))
    gate_grad = (inner_grad * up_act * sig * (1.0 + gate_act * (1.0 - sig))).astype(bf16)
    up_grad = (inner_grad * gate_act * sig).astype(bf16)
    gate_up_grad = lax.optimization_barrier(jnp.concatenate([gate_grad, up_grad], axis=1))
    mid_grad_part = dot_cols(gate_up_grad, gate_up).astype(bf16)
    gate_up_near, gate_up_far = scatter_seq_near(dot_rows(normed_mid, gate_up_grad), seq_here)
    mid_grad_in = scatter_ring(mid_grad_part)
    down_weight_part = dot_rows(inner, grad_all)
    gate_up_far = x.swap(gate_up_far, 2)
    mid_grad_in, down_weight_part, down_own, gate_up_far.value = lax.optimization_barrier(
        (mid_grad_in, down_weight_part, down_own, gate_up_far.value)
    )

    mid_scale = own_rows(mlp_scale)
    mid_unit = middle_own * mid_scale
    mid_term = mid_grad_in * gain2
    middle_grad = out_grad[0].astype(f32) + mid_scale * (
        mid_term - mid_unit * jnp.mean(mid_unit * mid_term, axis=-1, keepdims=True)
    )
    mlp_gain_part = jnp.sum(mid_grad_in * mid_unit, axis=0)
    middle_low = middle_grad.astype(bf16)
    att_grad = dot_cols(middle_low, full_out).astype(bf16)
    blocks = cut_columns((att_grad,), 1, None, ring())
    att_grad = lax.all_to_all(blocks, "ctx", 0, 0, tiled=True, axis_index_groups=[ring()])
    att_grad = att_grad.reshape(n * rows, -1)
    middle_low_all = gather_ring(middle_low)

    gate_up_sum = (gate_up_near + gate_up_far.value.astype(f32)).astype(bf16)
    att_grad, gate_up_sum = lax.optimization_barrier((att_grad, gate_up_sum))
    w_gate_up = lax.all_to_all(gate_up_sum.reshape(n, weight_rows, -1), "ctx", 0, 0, tiled=True)
    grads = [
        attention_back(
            *(m[:, halves[0]] for m in (query, key, value)), pos_all, att_first, lse_first, att_grad[:, halves[0]]
        )
    ]
    down_weight_near, down_weight_far = scatter_seq_near(down_weight_part, seq_here)
    att_grad, down_weight_far, grads[0] = lax.optimization_barrier(
        (att_grad, down_weight_far, grads[0])
    )
    down_weight_far = x.swap(down_weight_far, 2)
    grads.append(
        attention_back(
            *(m[:, halves[1]] for m in (query, key, value)), pos_all, att_second, lse_second, att_grad[:, halves[1]]
        )
    )
    query_acc, key_acc, value_acc = (jnp.concatenate(pair, axis=1) for pair in zip(*grads))
    qkv_grad = jnp.concatenate(
        [rotate(query_acc, cosine, -sine), rotate(key_acc, cosine, -sine), value_acc], axis=1
    ).astype(bf16)
    out_rows = w_out.shape[0]
    att_sub = jnp.concatenate(
        [
            lax.dynamic_slice_in_dim(att_low, (i * n + here) * out_rows, out_rows, 1)
            for i in range(seqs)
        ],
        axis=1,
    )
    w_out_near, w_out_far = scatter_seq_near(dot_rows(att_sub, middle_low_all), seq_here)
    hidden_out = (middle_own + down_own).astype(bf16)
    w_down_grad = down_weight_near + down_weight_far.value.astype(f32)
    qkv_grad, w_gate_up, w_down_grad, w_out_far = lax.optimization_barrier(
        (qkv_grad, w_gate_up, w_down_grad, w_out_far)
    )
    normed_grad_part = dot_cols(qkv_grad, qkv_sub)
    attn_gain_part = jnp.sum(normed_grad_part * (x_all * attn_scale), axis=0)
    beside = jnp.stack([attn_gain_part, mlp_gain_part], axis=1)
    beside = jnp.pad(beside, ((0, 0), (0, 126)))
    qkv_part = jnp.concatenate([dot_rows(normed, qkv_grad), beside], axis=1)
    qkv_near, qkv_far = scatter_seq_near(qkv_part, seq_here)
    normed_grad = scatter_ring(normed_grad_part.astype(bf16))
    qkv_far = Link("seq", 1).swap(qkv_far, 2)
    qkv_sum = (qkv_near + qkv_far.value.astype(f32)).astype(bf16)
    w_query_grad, w_key_grad, w_value_grad, gain_grads = to_owners(qkv_sum, 3, 1, 128)
    gain_grads = gain_grads.astype(f32).reshape(weight_rows, n, 128).sum(axis=1)
    w_out_grad = w_out_near + Link("seq", 1).swap(w_out_far, 2).value.astype(f32)
    w_out_grad, normed_grad = lax.optimization_barrier((w_out_grad, normed_grad))
    w_gate_grad, w_up_grad = paste_columns(w_gate_up, 2, seqs)

    own_scale = own_rows(attn_scale)
    own_unit = hidden_in[0].astype(f32) * own_scale
    attn_term = normed_grad * gain1
    hidden_grad = middle_grad + own_scale * (
        attn_term - own_unit * jnp.mean(own_unit * attn_term, axis=-1, keepdims=True)
    )
    return (
        hidden_out[None],
        hidden_grad[None],
        gain_grads[:, 0],
        w_query_grad,
        w_key_grad,
        w_value_grad,
        w_out_grad,
        gain_grads[:, 1],
        w_gate_grad,
        w_up_grad,
        w_down_grad,
    )


def solution(mesh):
    tokens = P("seq", "ctx", None)
    whole = P(("seq", "ctx"), None)
    gain = P(("seq", "ctx"))
    local = tuned if mesh.shape["ctx"] == 8 and mesh.shape["seq"] == 4 else plain
    return jax.shard_map(
        local,
        mesh=mesh,
        in_specs=(
            tokens,
            P("seq", "ctx"),
            gain,
            whole,
            whole,
            whole,
            whole,
            gain,
            whole,
            whole,
            whole,
            tokens,
        ),
        out_specs=(tokens, tokens, gain, whole, whole, whole, whole, gain, whole, whole, whole),
        check_vma=False,
    )
```

```python
import math

import jax
import jax.numpy as jnp
from jax import lax
from jax.experimental import pallas as pl
from jax.experimental.pallas import tpu as pltpu
from jax.sharding import PartitionSpec as P

HEADS = 32
HEAD_DIM = 64

eps = 1e-05
rope_base = 130000.0
mask_fill = -1e30
bf16 = jnp.bfloat16
f32 = jnp.float32


def plain_gather_ctx(block):
    return lax.all_gather(block, "ctx", axis=0, tiled=True)


def plain_gather_seq(block):
    return lax.all_gather(block, "seq", axis=0, tiled=True)


def plain_scatter_ctx(total):
    return lax.psum_scatter(total.astype(bf16), "ctx", scatter_dimension=0, tiled=True).astype(f32)


def plain_scatter_seq(total):
    return lax.psum_scatter(total.astype(bf16), "seq", scatter_dimension=0, tiled=True)


def plain_swap_ctx(blocks):
    return lax.all_to_all(blocks, "ctx", 0, 0, tiled=True)


def rms_scale(values):
    return lax.rsqrt(jnp.mean(values * values, axis=-1, keepdims=True) + eps)


def angle_table(positions):
    exponents = jnp.arange(HEAD_DIM // 2, dtype=f32) * (2.0 / HEAD_DIM)
    inverse = jnp.exp(-math.log(rope_base) * exponents)
    return positions.astype(f32)[:, None, None] * inverse[None, None, :]


def rotate(values, cosine, sine_part):
    half_dim = HEAD_DIM // 2
    heads = values.reshape(values.shape[0], -1, HEAD_DIM)
    first_half = heads[..., :half_dim]
    second_half = heads[..., half_dim:]
    return jnp.concatenate(
        [
            first_half * cosine - second_half * sine_part,
            second_half * cosine + first_half * sine_part,
        ],
        axis=-1,
    ).reshape(values.shape)


def dot(left, right):
    return jnp.dot(left, right, preferred_element_type=f32)


def dot_rows(left, right):
    return lax.dot_general(left, right, (((0,), (0,)), ((), ())), preferred_element_type=f32)


def dot_cols(left, right):
    return lax.dot_general(left, right, (((1,), (1,)), ((), ())), preferred_element_type=f32)


def columns_to_owners(weight, groups):
    n = lax.axis_size("ctx")
    rows = weight.shape[0]
    width = weight.shape[1] // (n * groups)
    blocks = weight.reshape(rows, groups, n, width).transpose(2, 0, 1, 3)
    mine = plain_swap_ctx(blocks.reshape(n, rows, groups * width))
    return plain_gather_seq(mine.reshape(n * rows, groups * width))


def columns_from_owners(total, groups):
    n = lax.axis_size("ctx")
    part = plain_scatter_seq(total)
    rows = part.shape[0] // n
    width = part.shape[1] // groups
    back = plain_swap_ctx(part.reshape(n, rows, groups * width))
    back = back.reshape(n, rows, groups, width).transpose(1, 2, 0, 3)
    return back.reshape(rows, groups * n * width)


def attention(query, key, value, positions):
    heads = query.shape[1] // HEAD_DIM
    scale = 1.0 / math.sqrt(HEAD_DIM)
    allowed = positions[None, None, :] <= positions[None, :, None]
    qh, kh, vh = (m.reshape(-1, heads, HEAD_DIM) for m in (query, key, value))
    scores = jnp.einsum("qhd,khd->hqk", qh, kh, preferred_element_type=f32) * scale
    scores = jnp.where(allowed, scores, mask_fill)
    row_max = jnp.max(scores, axis=-1)
    weights = jnp.exp(scores - row_max[:, :, None])
    row_total = jnp.sum(weights, axis=-1)
    mixed = jnp.einsum("hqk,khd->qhd", weights.astype(bf16), vh, preferred_element_type=f32)
    attended = mixed / row_total.T[:, :, None]
    return attended.reshape(query.shape), row_max + jnp.log(row_total)


def attention_back(query, key, value, positions, attended, lse, grad):
    heads = query.shape[1] // HEAD_DIM
    scale = 1.0 / math.sqrt(HEAD_DIM)
    allowed = positions[None, None, :] <= positions[None, :, None]
    qh, kh, vh, gh = (m.reshape(-1, heads, HEAD_DIM) for m in (query, key, value, grad))
    row_delta = jnp.sum(gh.astype(f32) * attended.reshape(-1, heads, HEAD_DIM), axis=-1)
    scores = jnp.einsum("qhd,khd->hqk", qh, kh, preferred_element_type=f32) * scale
    prob = jnp.where(allowed, jnp.exp(scores - lse[:, :, None]), 0.0)
    prob_grad = jnp.einsum("qhd,khd->hqk", gh, vh, preferred_element_type=f32)
    score_grad = (prob * (prob_grad - row_delta.T[:, :, None])).astype(bf16)
    prob_low = prob.astype(bf16)
    value_acc = jnp.einsum("hqk,qhd->khd", prob_low, gh, preferred_element_type=f32)
    query_acc = jnp.einsum("hqk,khd->qhd", score_grad, kh, preferred_element_type=f32) * scale
    key_acc = jnp.einsum("hqk,qhd->khd", score_grad, qh, preferred_element_type=f32) * scale
    return tuple(m.reshape(query.shape) for m in (query_acc, key_acc, value_acc))


def plain(
    hidden_in,
    positions,
    attn_gain,
    w_query,
    w_key,
    w_value,
    w_out,
    mlp_gain,
    w_gate,
    w_up,
    w_down,
    out_grad,
):
    n = lax.axis_size("ctx")
    seqs = lax.axis_size("seq")
    here = lax.axis_index("ctx")
    rows = hidden_in.shape[1]

    def own_rows(whole):
        return lax.dynamic_slice_in_dim(whole, here * rows, rows, 0)

    qkv_sub = columns_to_owners(jnp.concatenate([w_query, w_key, w_value], axis=1), 3)
    x_low = plain_gather_ctx(hidden_in[0])
    pos_all = plain_gather_ctx(positions[0])
    gains = lax.all_gather(jnp.stack([attn_gain, mlp_gain]), ("seq", "ctx"), axis=1, tiled=True)
    full_out = lax.all_gather(w_out, ("seq", "ctx"), axis=0, tiled=True)
    gate_up = columns_to_owners(jnp.concatenate([w_gate, w_up], axis=1), 2 * seqs)
    down_sub = plain_gather_seq(w_down)
    grad_all = plain_gather_ctx(out_grad[0])

    x = x_low.astype(f32)
    attn_scale = rms_scale(x)
    gain1 = gains[0].astype(f32)
    gain2 = gains[1].astype(f32)
    normed = (x * attn_scale * gain1).astype(bf16)
    angles = angle_table(pos_all)
    cosine, sine = jnp.cos(angles), jnp.sin(angles)
    qkv = dot(normed, qkv_sub)
    width = qkv.shape[1] // 3
    query = rotate(qkv[:, :width], cosine, sine).astype(bf16)
    key = rotate(qkv[:, width : 2 * width], cosine, sine).astype(bf16)
    value = qkv[:, 2 * width :].astype(bf16)
    attended, lse = attention(query, key, value, pos_all)
    att_low = lax.all_gather(attended.astype(bf16), "ctx", axis=1, tiled=True)

    middle = x + dot(att_low, full_out)
    mlp_scale = rms_scale(middle)
    normed_mid = (middle * mlp_scale * gain2).astype(bf16)
    gate_up_act = dot(normed_mid, gate_up)
    units = gate_up.shape[1] // 2
    gate_act, up_act = gate_up_act[:, :units], gate_up_act[:, units:]
    sig = jax.nn.sigmoid(gate_act)
    inner = (gate_act * sig * up_act).astype(bf16)
    middle_own = own_rows(middle)
    hidden_out = (middle_own + plain_scatter_ctx(dot(inner, down_sub))).astype(bf16)

    inner_grad = dot_cols(grad_all, down_sub)
    gate_grad = (inner_grad * up_act * sig * (1.0 + gate_act * (1.0 - sig))).astype(bf16)
    up_grad = (inner_grad * gate_act * sig).astype(bf16)
    gate_up_grad = jnp.concatenate([gate_grad, up_grad], axis=1)
    mid_grad_in = plain_scatter_ctx(dot_cols(gate_up_grad, gate_up))
    w_gate_up_grad = columns_from_owners(dot_rows(normed_mid, gate_up_grad), 2 * seqs).astype(f32)
    hidden_units = w_gate.shape[1]
    w_down_grad = plain_scatter_seq(dot_rows(inner, grad_all)).astype(f32)

    mid_scale = own_rows(mlp_scale)
    mid_unit = middle_own * mid_scale
    mid_term = mid_grad_in * gain2
    middle_grad = out_grad[0].astype(f32) + mid_scale * (
        mid_term - mid_unit * jnp.mean(mid_unit * mid_term, axis=-1, keepdims=True)
    )
    mlp_gain_part = jnp.sum(mid_grad_in * mid_unit, axis=0)
    middle_low = middle_grad.astype(bf16)
    att_grad = dot_cols(middle_low, full_out).astype(bf16)
    att_grad = plain_swap_ctx(att_grad.reshape(rows, n, -1).transpose(1, 0, 2)).reshape(n * rows, -1)
    middle_low_all = plain_gather_ctx(middle_low)
    out_rows = w_out.shape[0]
    att_cols = att_low.reshape(n * rows, seqs, n, out_rows)
    att_sub = lax.dynamic_slice_in_dim(att_cols, here, 1, 2).reshape(n * rows, seqs * out_rows)
    w_out_grad = plain_scatter_seq(dot_rows(att_sub, middle_low_all)).astype(f32)

    query_acc, key_acc, value_acc = attention_back(
        query, key, value, pos_all, attended, lse, att_grad
    )
    qkv_grad = jnp.concatenate(
        [rotate(query_acc, cosine, -sine), rotate(key_acc, cosine, -sine), value_acc], axis=1
    ).astype(bf16)
    normed_grad = plain_scatter_ctx(dot_cols(qkv_grad, qkv_sub))
    own_scale = own_rows(attn_scale)
    own_unit = hidden_in[0].astype(f32) * own_scale
    attn_term = normed_grad * gain1
    hidden_grad = middle_grad + own_scale * (
        attn_term - own_unit * jnp.mean(own_unit * attn_term, axis=-1, keepdims=True)
    )
    attn_gain_part = jnp.sum(normed_grad * own_unit, axis=0)
    w_qkv_grad = columns_from_owners(dot_rows(normed, qkv_grad), 3).astype(f32)
    model_width = x.shape[1]
    gain_grads = lax.psum_scatter(
        jnp.stack([attn_gain_part, mlp_gain_part], axis=1),
        ("seq", "ctx"),
        scatter_dimension=0,
        tiled=True,
    )
    return (
        hidden_out[None],
        hidden_grad[None],
        gain_grads[:, 0],
        w_qkv_grad[:, :model_width],
        w_qkv_grad[:, model_width : 2 * model_width],
        w_qkv_grad[:, 2 * model_width :],
        w_out_grad,
        gain_grads[:, 1],
        w_gate_up_grad[:, :hidden_units],
        w_gate_up_grad[:, hidden_units:],
        w_down_grad,
    )


class Box:
    def __init__(self, value):
        self.value = value


def value_of(block):
    return block.value if isinstance(block, Box) else block


def order(block, *boxes):
    values = lax.optimization_barrier((value_of(block),) + tuple(box.value for box in boxes))
    for box, value in zip(boxes, values[1:]):
        box.value = value
    return values[0]


class Link:
    def __init__(self, axis, depth):
        self.axis = axis
        self.depth = depth
        self.arrived = []

    def swap(self, block, mask):
        n = lax.axis_size(self.axis)
        if len(self.arrived) >= self.depth:
            before = order(block, self.arrived[-self.depth])
            if isinstance(block, Box):
                block.value = before
            block = before
        got = Box(lax.ppermute(value_of(block), self.axis, [(i, i ^ mask) for i in range(n)]))
        self.arrived.append(got)
        return got


def place(pieces, places, inner=(0,)):
    pieces = [value_of(piece) for piece in pieces]
    rows, width = pieces[0].shape
    count = len(pieces)
    shape = (count * rows, width)

    def kernel(places_ref, *refs):
        parts, whole, sems = refs[:count], refs[count], refs[count + 1]
        copies = []
        for i in range(count):
            for j, to in enumerate(inner):
                cut = rows // len(inner)
                start = pl.multiple_of(places_ref[i] * rows + to * cut, cut)
                copies.append(
                    pltpu.make_async_copy(
                        parts[i].at[pl.ds(j * cut, cut), :],
                        whole.at[pl.ds(start, cut), :],
                        sems.at[i * len(inner) + j],
                    )
                )
        for copy in copies:
            copy.start()
        for copy in copies:
            copy.wait()

    return pl.pallas_call(
        kernel,
        out_shape=jax.ShapeDtypeStruct(shape, pieces[0].dtype),
        in_specs=[pl.BlockSpec(memory_space=pltpu.SMEM)]
        + [pl.BlockSpec(memory_space=pl.ANY)] * count,
        out_specs=pl.BlockSpec(memory_space=pltpu.VMEM),
        scratch_shapes=[pltpu.SemaphoreType.DMA((count * len(inner),))],
        compiler_params=pltpu.CompilerParams(vmem_limit_bytes=32 * 1024 * 1024),
        cost_estimate=pl.CostEstimate(flops=0, bytes_accessed=4 * rows * width * count, transcendentals=0),
    )(jnp.stack(places).astype(jnp.int32), *pieces)


def cut_columns(weights, groups, beside, devices=None):
    n = lax.axis_size("ctx")
    rows = weights[0].shape[0]
    width = weights[0].shape[1] // (n * groups)
    arrays = list(weights) + ([] if beside is None else [beside])
    total = len(weights) * groups * width + (0 if beside is None else beside.shape[1])

    def kernel(*refs):
        out = refs[-1]
        for i, device in enumerate(devices or range(n)):
            at = 0
            for weight in refs[: len(weights)]:
                for group in range(groups):
                    start = (group * n + device) * width
                    out[i, :, at : at + width] = weight[:, start : start + width]
                    at += width
            if beside is not None:
                out[i, :, at:] = refs[len(weights)][...]

    vmem = pl.BlockSpec(memory_space=pltpu.VMEM)
    return pl.pallas_call(
        kernel,
        out_shape=jax.ShapeDtypeStruct((n, rows, total), bf16),
        in_specs=[vmem] * len(arrays),
        out_specs=vmem,
        compiler_params=pltpu.CompilerParams(vmem_limit_bytes=32 * 1024 * 1024),
    )(*arrays)


def paste_columns(blocks, count, groups, beside=0):
    n, rows, total = blocks.shape
    width = (total - beside) // (count * groups)
    shapes = [jax.ShapeDtypeStruct((rows, groups * n * width), f32)] * count
    if beside:
        shapes.append(jax.ShapeDtypeStruct((rows, n * beside), f32))

    def kernel(ref, *outs):
        for device in range(n):
            at = 0
            for i in range(count):
                for group in range(groups):
                    start = (group * n + device) * width
                    outs[i][:, start : start + width] = ref[device, :, at : at + width].astype(f32)
                    at += width
            if beside:
                start = device * beside
                outs[count][:, start : start + beside] = ref[device, :, at:].astype(f32)

    vmem = pl.BlockSpec(memory_space=pltpu.VMEM)
    return pl.pallas_call(
        kernel,
        out_shape=shapes,
        in_specs=[vmem],
        out_specs=[vmem] * len(shapes),
        compiler_params=pltpu.CompilerParams(vmem_limit_bytes=32 * 1024 * 1024),
    )(blocks)


def ring():
    n = lax.axis_size("ctx")
    return list(range(0, n, 2)) + list(range(n - 1, 0, -2))


def gather_ring(block):
    return lax.all_gather(block, "ctx", axis=0, tiled=True, axis_index_groups=[ring()])


def scatter_ring(total):
    return lax.psum_scatter(
        total, "ctx", scatter_dimension=0, tiled=True, axis_index_groups=[ring()]
    ).astype(f32)


def rearranged(stack, places, columns=False):
    count = len(places)
    rows, width = stack.shape[0] // count, stack.shape[1]

    def kernel(stack_ref, whole, sems):
        copies = []
        for i, to in enumerate(places):
            if columns:
                there = whole.at[:, pl.ds(to * width, width)]
            else:
                there = whole.at[pl.ds(to * rows, rows), :]
            block = stack_ref.at[pl.ds(i * rows, rows), :]
            copies.append(pltpu.make_async_copy(block, there, sems.at[i]))
        for copy in copies:
            copy.start()
        for copy in copies:
            copy.wait()

    shape = (rows, count * width) if columns else stack.shape
    return pl.pallas_call(
        kernel,
        out_shape=jax.ShapeDtypeStruct(shape, stack.dtype),
        in_specs=[pl.BlockSpec(memory_space=pl.ANY)],
        out_specs=pl.BlockSpec(memory_space=pltpu.VMEM),
        scratch_shapes=[pltpu.SemaphoreType.DMA((count,))],
        compiler_params=pltpu.CompilerParams(vmem_limit_bytes=32 * 1024 * 1024),
    )(stack)


def core_swap(block):
    n = lax.axis_size("seq")
    return Box(lax.ppermute(value_of(block), "seq", [(i, i ^ 1) for i in range(n)]))


def gather_seq(x, block):
    far = x.swap(block, 2)
    return [(0, block), (1, core_swap(block)), (2, far), (3, core_swap(far))]


def scatter_seq_near(total, here):
    rows = total.shape[0] // 4

    def piece(offset):
        return lax.dynamic_slice_in_dim(total, (here ^ offset) * rows, rows, 0)

    got = core_swap(jnp.concatenate([piece(3), piece(1)], axis=0).astype(bf16))
    return piece(0) + got.value[rows:].astype(f32), (
        piece(2) + got.value[:rows].astype(f32)
    ).astype(bf16)


def to_owners(part, count, groups, beside=0):
    n = lax.axis_size("ctx")
    blocks = lax.all_to_all(part.reshape(n, -1, part.shape[1]), "ctx", 0, 0, tiled=True)
    return paste_columns(blocks, count, groups, beside)


def tuned(
    hidden_in,
    positions,
    attn_gain,
    w_query,
    w_key,
    w_value,
    w_out,
    mlp_gain,
    w_gate,
    w_up,
    w_down,
    out_grad,
):
    n = lax.axis_size("ctx")
    seqs = lax.axis_size("seq")
    here = lax.axis_index("ctx")
    seq_here = lax.axis_index("seq")
    rows = hidden_in.shape[1]
    weight_rows = w_query.shape[0]
    x = Link("seq", 1)
    place_here = jnp.where(here % 2 == 0, here // 2, n - 1 - here // 2)

    def own_rows(whole):
        return lax.dynamic_slice_in_dim(whole, place_here * rows, rows, 0)

    def from_devices(held):
        return place([part for _, part in held], [seq_here ^ o for o, _ in held])

    own_pos = positions[0].reshape(weight_rows, -1)
    per_row = own_pos.shape[1]
    beside = jnp.concatenate(
        [
            attn_gain[:, None],
            mlp_gain[:, None],
            (own_pos // 64).astype(bf16),
            (own_pos % 64).astype(bf16),
        ],
        axis=1,
    )
    beside = jnp.pad(beside, ((0, 0), (0, 128 - beside.shape[1])))
    x_low = gather_ring(hidden_in[0])
    down_steps = gather_seq(Link("seq", 1), w_down)
    blocks = cut_columns((w_query, w_key, w_value), 1, beside)
    qkv_mine = lax.all_to_all(blocks, "ctx", 0, 0, tiled=True).reshape(n * weight_rows, -1)
    down_far = down_steps[2][1]
    late_out, late_gate, late_up, qkv_mine, down_far.value = lax.optimization_barrier(
        (w_out, w_gate, w_up, qkv_mine, down_far.value)
    )
    qkv_steps = gather_seq(x, qkv_mine)
    out_ring = gather_ring(late_out)
    blocks = cut_columns((late_gate, late_up), seqs, None)
    gate_up = lax.all_to_all(blocks, "ctx", 0, 0, tiled=True).reshape(n * weight_rows, -1)
    qkv_sub = from_devices(qkv_steps)
    down_sub = from_devices(down_steps)
    pos_cuts = qkv_mine[:, -128:].astype(jnp.int32)
    pos_all = pos_cuts[:, 2 : 2 + per_row] * 64 + pos_cuts[:, 2 + per_row : 2 + 2 * per_row]
    pos_all = pos_all.reshape(n, rows)
    pos_all = jnp.concatenate([pos_all[device] for device in ring()])
    gain1 = qkv_sub[:, -128].astype(f32)
    gain2 = qkv_sub[:, -127].astype(f32)
    qkv_sub = qkv_sub[:, :-128]

    x_all = x_low.astype(f32)
    attn_scale = rms_scale(x_all)
    normed = (x_all * attn_scale * gain1).astype(bf16)
    angles = angle_table(pos_all)
    cosine, sine = jnp.cos(angles), jnp.sin(angles)
    qkv = dot(normed, qkv_sub)
    width = qkv.shape[1] // 3
    query = rotate(qkv[:, :width], cosine, sine).astype(bf16)
    key = rotate(qkv[:, width : 2 * width], cosine, sine).astype(bf16)
    value = qkv[:, 2 * width :].astype(bf16)
    split = width // 2
    halves = [slice(0, split), slice(split, width)]
    att_first, lse_first = attention(*(m[:, halves[0]] for m in (query, key, value)), pos_all)
    value, gate_up = lax.optimization_barrier((value, gate_up))
    att_second, lse_second = attention(*(m[:, halves[1]] for m in (query, key, value)), pos_all)
    att_low = jnp.concatenate([att_first, att_second], axis=1).astype(bf16)
    cut = gate_up.shape[0] // 2
    parts = [gate_up[:cut], gate_up[cut:]]
    far = [x.swap(parts[0], 2)]
    att_low, out_ring, far[0].value = lax.optimization_barrier((att_low, out_ring, far[0].value))
    att_stack = gather_ring(att_low)
    out_steps = gather_seq(x, out_ring)
    far.append(x.swap(parts[1], 2))
    full_out = place([part for _, part in out_steps], [seq_here ^ o for o, _ in out_steps], ring())
    late_grad, att_stack = lax.optimization_barrier((out_grad[0], att_stack))
    grad_all = gather_ring(late_grad)
    att_stack, full_out, down_sub = lax.optimization_barrier((att_stack, full_out, down_sub))
    att_low = rearranged(att_stack, ring(), columns=True)

    middle = x_all + dot(att_low, full_out)
    mlp_scale = rms_scale(middle)
    normed_mid = (middle * mlp_scale * gain2).astype(bf16)
    normed_mid, far[1].value = lax.optimization_barrier((normed_mid, far[1].value))
    held = []
    for part, other in zip(parts, far):
        held += [(0, part), (1, core_swap(part)), (2, other), (3, core_swap(other))]
    gate_up = place(
        [part for _, part in held],
        [(seq_here ^ o) * 2 + i // 4 for i, (o, _) in enumerate(held)],
    )
    gate_up_act = dot(normed_mid, gate_up)
    units = gate_up.shape[1] // 2
    gate_act, up_act = gate_up_act[:, :units], gate_up_act[:, units:]
    sig = jax.nn.sigmoid(gate_act)
    inner = (gate_act * sig * up_act).astype(bf16)
    middle_own = own_rows(middle)

    down_part = dot(inner, down_sub).astype(bf16)
    grad_all, down_part = lax.optimization_barrier((grad_all, down_part))
    down_own = scatter_ring(down_part)
    inner_grad = lax.optimization_barrier(dot_cols(grad_all, down_sub))
    gate_grad = (inner_grad * up_act * sig * (1.0 + gate_act * (1.0 - sig))).astype(bf16)
    up_grad = (inner_grad * gate_act * sig).astype(bf16)
    gate_up_grad = lax.optimization_barrier(jnp.concatenate([gate_grad, up_grad], axis=1))
    mid_grad_part = dot_cols(gate_up_grad, gate_up).astype(bf16)
    gate_up_near, gate_up_far = scatter_seq_near(dot_rows(normed_mid, gate_up_grad), seq_here)
    mid_grad_in = scatter_ring(mid_grad_part)
    down_weight_part = dot_rows(inner, grad_all)
    gate_up_far = x.swap(gate_up_far, 2)
    mid_grad_in, down_weight_part, down_own, gate_up_far.value = lax.optimization_barrier(
        (mid_grad_in, down_weight_part, down_own, gate_up_far.value)
    )

    mid_scale = own_rows(mlp_scale)
    mid_unit = middle_own * mid_scale
    mid_term = mid_grad_in * gain2
    middle_grad = out_grad[0].astype(f32) + mid_scale * (
        mid_term - mid_unit * jnp.mean(mid_unit * mid_term, axis=-1, keepdims=True)
    )
    mlp_gain_part = jnp.sum(mid_grad_in * mid_unit, axis=0)
    middle_low = middle_grad.astype(bf16)
    att_grad = dot_cols(middle_low, full_out).astype(bf16)
    blocks = cut_columns((att_grad,), 1, None, ring())
    att_grad = lax.all_to_all(blocks, "ctx", 0, 0, tiled=True, axis_index_groups=[ring()])
    att_grad = att_grad.reshape(n * rows, -1)
    middle_low_all = gather_ring(middle_low)

    gate_up_sum = (gate_up_near + gate_up_far.value.astype(f32)).astype(bf16)
    att_grad, gate_up_sum = lax.optimization_barrier((att_grad, gate_up_sum))
    gate_sum, up_sum = (
        lax.all_to_all(part.reshape(n, weight_rows, -1), "ctx", 0, 0, tiled=True)
        for part in (gate_up_sum[:, :units], gate_up_sum[:, units:])
    )
    grads = [
        attention_back(
            *(m[:, halves[0]] for m in (query, key, value)), pos_all, att_first, lse_first, att_grad[:, halves[0]]
        )
    ]
    down_weight_near, down_weight_far = scatter_seq_near(down_weight_part, seq_here)
    att_grad, down_weight_far, grads[0] = lax.optimization_barrier(
        (att_grad, down_weight_far, grads[0])
    )
    down_weight_far = x.swap(down_weight_far, 2)
    grads.append(
        attention_back(
            *(m[:, halves[1]] for m in (query, key, value)), pos_all, att_second, lse_second, att_grad[:, halves[1]]
        )
    )
    query_acc, key_acc, value_acc = (jnp.concatenate(pair, axis=1) for pair in zip(*grads))
    qkv_grad = jnp.concatenate(
        [rotate(query_acc, cosine, -sine), rotate(key_acc, cosine, -sine), value_acc], axis=1
    ).astype(bf16)
    out_rows = w_out.shape[0]
    att_sub = jnp.concatenate(
        [
            lax.dynamic_slice_in_dim(att_low, (i * n + here) * out_rows, out_rows, 1)
            for i in range(seqs)
        ],
        axis=1,
    )
    w_out_near, w_out_far = scatter_seq_near(dot_rows(att_sub, middle_low_all), seq_here)
    hidden_out = (middle_own + down_own).astype(bf16)
    qkv_grad, gate_sum = lax.optimization_barrier((qkv_grad, gate_sum))
    normed_grad_part = dot_cols(qkv_grad, qkv_sub)
    attn_gain_part = jnp.sum(normed_grad_part * (x_all * attn_scale), axis=0)
    beside = jnp.stack([attn_gain_part, mlp_gain_part], axis=1)
    beside = jnp.pad(beside, ((0, 0), (0, 126)))
    qkv_part = jnp.concatenate([dot_rows(normed, qkv_grad), beside], axis=1)
    qkv_near, qkv_far = scatter_seq_near(qkv_part, seq_here)
    normed_grad = scatter_ring(normed_grad_part.astype(bf16))
    qkv_far = Link("seq", 1).swap(qkv_far, 2)
    qkv_far.value, up_sum, w_out_far = lax.optimization_barrier((qkv_far.value, up_sum, w_out_far))
    qkv_sum = (qkv_near + qkv_far.value.astype(f32)).astype(bf16)
    w_query_grad, w_key_grad, w_value_grad, gain_grads = to_owners(qkv_sum, 3, 1, 128)
    gain_grads = gain_grads.astype(f32).reshape(weight_rows, n, 128).sum(axis=1)
    w_out_grad = w_out_near + Link("seq", 1).swap(w_out_far, 2).value.astype(f32)
    w_down_grad = down_weight_near + down_weight_far.value.astype(f32)
    w_out_grad, w_down_grad, normed_grad = lax.optimization_barrier(
        (w_out_grad, w_down_grad, normed_grad)
    )
    (w_gate_grad,) = paste_columns(gate_sum, 1, seqs)
    (w_up_grad,) = paste_columns(up_sum, 1, seqs)

    own_scale = own_rows(attn_scale)
    own_unit = hidden_in[0].astype(f32) * own_scale
    attn_term = normed_grad * gain1
    hidden_grad = middle_grad + own_scale * (
        attn_term - own_unit * jnp.mean(own_unit * attn_term, axis=-1, keepdims=True)
    )
    return (
        hidden_out[None],
        hidden_grad[None],
        gain_grads[:, 0],
        w_query_grad,
        w_key_grad,
        w_value_grad,
        w_out_grad,
        gain_grads[:, 1],
        w_gate_grad,
        w_up_grad,
        w_down_grad,
    )


def solution(mesh):
    tokens = P("seq", "ctx", None)
    whole = P(("seq", "ctx"), None)
    gain = P(("seq", "ctx"))
    local = tuned if mesh.shape["ctx"] == 8 and mesh.shape["seq"] == 4 else plain
    return jax.shard_map(
        local,
        mesh=mesh,
        in_specs=(
            tokens,
            P("seq", "ctx"),
            gain,
            whole,
            whole,
            whole,
            whole,
            gain,
            whole,
            whole,
            whole,
            tokens,
        ),
        out_specs=(tokens, tokens, gain, whole, whole, whole, whole, gain, whole, whole, whole),
        check_vma=False,
    )
```

```python
import math

import jax
import jax.numpy as jnp
from jax import lax
from jax.experimental import pallas as pl
from jax.experimental.pallas import tpu as pltpu
from jax.sharding import PartitionSpec as P

HEADS = 32
HEAD_DIM = 64

eps = 1e-05
rope_base = 130000.0
mask_fill = -1e30
bf16 = jnp.bfloat16
f32 = jnp.float32


def plain_gather_ctx(block):
    return lax.all_gather(block, "ctx", axis=0, tiled=True)


def plain_gather_seq(block):
    return lax.all_gather(block, "seq", axis=0, tiled=True)


def plain_scatter_ctx(total):
    return lax.psum_scatter(total.astype(bf16), "ctx", scatter_dimension=0, tiled=True).astype(f32)


def plain_scatter_seq(total):
    return lax.psum_scatter(total.astype(bf16), "seq", scatter_dimension=0, tiled=True)


def plain_swap_ctx(blocks):
    return lax.all_to_all(blocks, "ctx", 0, 0, tiled=True)


def rms_scale(values):
    return lax.rsqrt(jnp.mean(values * values, axis=-1, keepdims=True) + eps)


def angle_table(positions):
    exponents = jnp.arange(HEAD_DIM // 2, dtype=f32) * (2.0 / HEAD_DIM)
    inverse = jnp.exp(-math.log(rope_base) * exponents)
    return positions.astype(f32)[:, None, None] * inverse[None, None, :]


def rotate(values, cosine, sine_part):
    half_dim = HEAD_DIM // 2
    heads = values.reshape(values.shape[0], -1, HEAD_DIM)
    first_half = heads[..., :half_dim]
    second_half = heads[..., half_dim:]
    return jnp.concatenate(
        [
            first_half * cosine - second_half * sine_part,
            second_half * cosine + first_half * sine_part,
        ],
        axis=-1,
    ).reshape(values.shape)


def dot(left, right):
    return jnp.dot(left, right, preferred_element_type=f32)


def dot_rows(left, right):
    return lax.dot_general(left, right, (((0,), (0,)), ((), ())), preferred_element_type=f32)


def dot_cols(left, right):
    return lax.dot_general(left, right, (((1,), (1,)), ((), ())), preferred_element_type=f32)


def columns_to_owners(weight, groups):
    n = lax.axis_size("ctx")
    rows = weight.shape[0]
    width = weight.shape[1] // (n * groups)
    blocks = weight.reshape(rows, groups, n, width).transpose(2, 0, 1, 3)
    mine = plain_swap_ctx(blocks.reshape(n, rows, groups * width))
    return plain_gather_seq(mine.reshape(n * rows, groups * width))


def columns_from_owners(total, groups):
    n = lax.axis_size("ctx")
    part = plain_scatter_seq(total)
    rows = part.shape[0] // n
    width = part.shape[1] // groups
    back = plain_swap_ctx(part.reshape(n, rows, groups * width))
    back = back.reshape(n, rows, groups, width).transpose(1, 2, 0, 3)
    return back.reshape(rows, groups * n * width)


def attention(query, key, value, positions):
    heads = query.shape[1] // HEAD_DIM
    scale = 1.0 / math.sqrt(HEAD_DIM)
    allowed = positions[None, None, :] <= positions[None, :, None]
    qh, kh, vh = (m.reshape(-1, heads, HEAD_DIM) for m in (query, key, value))
    scores = jnp.einsum("qhd,khd->hqk", qh, kh, preferred_element_type=f32) * scale
    scores = jnp.where(allowed, scores, mask_fill)
    row_max = jnp.max(scores, axis=-1)
    weights = jnp.exp(scores - row_max[:, :, None])
    row_total = jnp.sum(weights, axis=-1)
    mixed = jnp.einsum("hqk,khd->qhd", weights.astype(bf16), vh, preferred_element_type=f32)
    attended = mixed / row_total.T[:, :, None]
    return attended.reshape(query.shape), row_max + jnp.log(row_total)


def attention_back(query, key, value, positions, attended, lse, grad):
    heads = query.shape[1] // HEAD_DIM
    scale = 1.0 / math.sqrt(HEAD_DIM)
    allowed = positions[None, None, :] <= positions[None, :, None]
    qh, kh, vh, gh = (m.reshape(-1, heads, HEAD_DIM) for m in (query, key, value, grad))
    row_delta = jnp.sum(gh.astype(f32) * attended.reshape(-1, heads, HEAD_DIM), axis=-1)
    scores = jnp.einsum("qhd,khd->hqk", qh, kh, preferred_element_type=f32) * scale
    prob = jnp.where(allowed, jnp.exp(scores - lse[:, :, None]), 0.0)
    prob_grad = jnp.einsum("qhd,khd->hqk", gh, vh, preferred_element_type=f32)
    score_grad = (prob * (prob_grad - row_delta.T[:, :, None])).astype(bf16)
    prob_low = prob.astype(bf16)
    value_acc = jnp.einsum("hqk,qhd->khd", prob_low, gh, preferred_element_type=f32)
    query_acc = jnp.einsum("hqk,khd->qhd", score_grad, kh, preferred_element_type=f32) * scale
    key_acc = jnp.einsum("hqk,qhd->khd", score_grad, qh, preferred_element_type=f32) * scale
    return tuple(m.reshape(query.shape) for m in (query_acc, key_acc, value_acc))


def plain(
    hidden_in,
    positions,
    attn_gain,
    w_query,
    w_key,
    w_value,
    w_out,
    mlp_gain,
    w_gate,
    w_up,
    w_down,
    out_grad,
):
    n = lax.axis_size("ctx")
    seqs = lax.axis_size("seq")
    here = lax.axis_index("ctx")
    rows = hidden_in.shape[1]

    def own_rows(whole):
        return lax.dynamic_slice_in_dim(whole, here * rows, rows, 0)

    qkv_sub = columns_to_owners(jnp.concatenate([w_query, w_key, w_value], axis=1), 3)
    x_low = plain_gather_ctx(hidden_in[0])
    pos_all = plain_gather_ctx(positions[0])
    gains = lax.all_gather(jnp.stack([attn_gain, mlp_gain]), ("seq", "ctx"), axis=1, tiled=True)
    full_out = lax.all_gather(w_out, ("seq", "ctx"), axis=0, tiled=True)
    gate_up = columns_to_owners(jnp.concatenate([w_gate, w_up], axis=1), 2 * seqs)
    down_sub = plain_gather_seq(w_down)
    grad_all = plain_gather_ctx(out_grad[0])

    x = x_low.astype(f32)
    attn_scale = rms_scale(x)
    gain1 = gains[0].astype(f32)
    gain2 = gains[1].astype(f32)
    normed = (x * attn_scale * gain1).astype(bf16)
    angles = angle_table(pos_all)
    cosine, sine = jnp.cos(angles), jnp.sin(angles)
    qkv = dot(normed, qkv_sub)
    width = qkv.shape[1] // 3
    query = rotate(qkv[:, :width], cosine, sine).astype(bf16)
    key = rotate(qkv[:, width : 2 * width], cosine, sine).astype(bf16)
    value = qkv[:, 2 * width :].astype(bf16)
    attended, lse = attention(query, key, value, pos_all)
    att_low = lax.all_gather(attended.astype(bf16), "ctx", axis=1, tiled=True)

    middle = x + dot(att_low, full_out)
    mlp_scale = rms_scale(middle)
    normed_mid = (middle * mlp_scale * gain2).astype(bf16)
    gate_up_act = dot(normed_mid, gate_up)
    units = gate_up.shape[1] // 2
    gate_act, up_act = gate_up_act[:, :units], gate_up_act[:, units:]
    sig = jax.nn.sigmoid(gate_act)
    inner = (gate_act * sig * up_act).astype(bf16)
    middle_own = own_rows(middle)
    hidden_out = (middle_own + plain_scatter_ctx(dot(inner, down_sub))).astype(bf16)

    inner_grad = dot_cols(grad_all, down_sub)
    gate_grad = (inner_grad * up_act * sig * (1.0 + gate_act * (1.0 - sig))).astype(bf16)
    up_grad = (inner_grad * gate_act * sig).astype(bf16)
    gate_up_grad = jnp.concatenate([gate_grad, up_grad], axis=1)
    mid_grad_in = plain_scatter_ctx(dot_cols(gate_up_grad, gate_up))
    w_gate_up_grad = columns_from_owners(dot_rows(normed_mid, gate_up_grad), 2 * seqs).astype(f32)
    hidden_units = w_gate.shape[1]
    w_down_grad = plain_scatter_seq(dot_rows(inner, grad_all)).astype(f32)

    mid_scale = own_rows(mlp_scale)
    mid_unit = middle_own * mid_scale
    mid_term = mid_grad_in * gain2
    middle_grad = out_grad[0].astype(f32) + mid_scale * (
        mid_term - mid_unit * jnp.mean(mid_unit * mid_term, axis=-1, keepdims=True)
    )
    mlp_gain_part = jnp.sum(mid_grad_in * mid_unit, axis=0)
    middle_low = middle_grad.astype(bf16)
    att_grad = dot_cols(middle_low, full_out).astype(bf16)
    att_grad = plain_swap_ctx(att_grad.reshape(rows, n, -1).transpose(1, 0, 2)).reshape(n * rows, -1)
    middle_low_all = plain_gather_ctx(middle_low)
    out_rows = w_out.shape[0]
    att_cols = att_low.reshape(n * rows, seqs, n, out_rows)
    att_sub = lax.dynamic_slice_in_dim(att_cols, here, 1, 2).reshape(n * rows, seqs * out_rows)
    w_out_grad = plain_scatter_seq(dot_rows(att_sub, middle_low_all)).astype(f32)

    query_acc, key_acc, value_acc = attention_back(
        query, key, value, pos_all, attended, lse, att_grad
    )
    qkv_grad = jnp.concatenate(
        [rotate(query_acc, cosine, -sine), rotate(key_acc, cosine, -sine), value_acc], axis=1
    ).astype(bf16)
    normed_grad = plain_scatter_ctx(dot_cols(qkv_grad, qkv_sub))
    own_scale = own_rows(attn_scale)
    own_unit = hidden_in[0].astype(f32) * own_scale
    attn_term = normed_grad * gain1
    hidden_grad = middle_grad + own_scale * (
        attn_term - own_unit * jnp.mean(own_unit * attn_term, axis=-1, keepdims=True)
    )
    attn_gain_part = jnp.sum(normed_grad * own_unit, axis=0)
    w_qkv_grad = columns_from_owners(dot_rows(normed, qkv_grad), 3).astype(f32)
    model_width = x.shape[1]
    gain_grads = lax.psum_scatter(
        jnp.stack([attn_gain_part, mlp_gain_part], axis=1),
        ("seq", "ctx"),
        scatter_dimension=0,
        tiled=True,
    )
    return (
        hidden_out[None],
        hidden_grad[None],
        gain_grads[:, 0],
        w_qkv_grad[:, :model_width],
        w_qkv_grad[:, model_width : 2 * model_width],
        w_qkv_grad[:, 2 * model_width :],
        w_out_grad,
        gain_grads[:, 1],
        w_gate_up_grad[:, :hidden_units],
        w_gate_up_grad[:, hidden_units:],
        w_down_grad,
    )


class Box:
    def __init__(self, value):
        self.value = value


def value_of(block):
    return block.value if isinstance(block, Box) else block


def order(block, *boxes):
    values = lax.optimization_barrier((value_of(block),) + tuple(box.value for box in boxes))
    for box, value in zip(boxes, values[1:]):
        box.value = value
    return values[0]


class Link:
    def __init__(self, axis, depth):
        self.axis = axis
        self.depth = depth
        self.arrived = []

    def swap(self, block, mask):
        n = lax.axis_size(self.axis)
        if len(self.arrived) >= self.depth:
            before = order(block, self.arrived[-self.depth])
            if isinstance(block, Box):
                block.value = before
            block = before
        got = Box(lax.ppermute(value_of(block), self.axis, [(i, i ^ mask) for i in range(n)]))
        self.arrived.append(got)
        return got


def place(pieces, places, inner=(0,)):
    pieces = [value_of(piece) for piece in pieces]
    rows, width = pieces[0].shape
    count = len(pieces)
    shape = (count * rows, width)

    def kernel(places_ref, *refs):
        parts, whole, sems = refs[:count], refs[count], refs[count + 1]
        copies = []
        for i in range(count):
            for j, to in enumerate(inner):
                cut = rows // len(inner)
                start = pl.multiple_of(places_ref[i] * rows + to * cut, cut)
                copies.append(
                    pltpu.make_async_copy(
                        parts[i].at[pl.ds(j * cut, cut), :],
                        whole.at[pl.ds(start, cut), :],
                        sems.at[i * len(inner) + j],
                    )
                )
        for copy in copies:
            copy.start()
        for copy in copies:
            copy.wait()

    return pl.pallas_call(
        kernel,
        out_shape=jax.ShapeDtypeStruct(shape, pieces[0].dtype),
        in_specs=[pl.BlockSpec(memory_space=pltpu.SMEM)]
        + [pl.BlockSpec(memory_space=pl.ANY)] * count,
        out_specs=pl.BlockSpec(memory_space=pltpu.VMEM),
        scratch_shapes=[pltpu.SemaphoreType.DMA((count * len(inner),))],
        compiler_params=pltpu.CompilerParams(vmem_limit_bytes=32 * 1024 * 1024),
        cost_estimate=pl.CostEstimate(flops=0, bytes_accessed=4 * rows * width * count, transcendentals=0),
    )(jnp.stack(places).astype(jnp.int32), *pieces)


def place_pairs(stacks, places, inner):
    count = len(inner)
    rows, width = stacks[0].shape[0] // (2 * count), stacks[0].shape[1]

    def kernel(places_ref, *refs):
        parts, whole, sems = refs[: len(stacks)], refs[len(stacks)], refs[len(stacks) + 1]
        copies = []
        for p, part in enumerate(parts):
            for i, to in enumerate(inner):
                for e in range(2):
                    start = places_ref[2 * p + e] * (count * rows) + to * rows
                    copies.append(
                        pltpu.make_async_copy(
                            part.at[pl.ds((2 * i + e) * rows, rows), :],
                            whole.at[pl.ds(pl.multiple_of(start, rows), rows), :],
                            sems.at[len(copies)],
                        )
                    )
        for copy in copies:
            copy.start()
        for copy in copies:
            copy.wait()

    return pl.pallas_call(
        kernel,
        out_shape=jax.ShapeDtypeStruct((2 * len(stacks) * count * rows, width), stacks[0].dtype),
        in_specs=[pl.BlockSpec(memory_space=pltpu.SMEM)]
        + [pl.BlockSpec(memory_space=pl.ANY)] * len(stacks),
        out_specs=pl.BlockSpec(memory_space=pltpu.VMEM),
        scratch_shapes=[pltpu.SemaphoreType.DMA((2 * len(stacks) * count,))],
        compiler_params=pltpu.CompilerParams(vmem_limit_bytes=32 * 1024 * 1024),
    )(jnp.stack(places).astype(jnp.int32), *stacks)


def cut_columns(weights, groups, beside, devices=None):
    n = lax.axis_size("ctx")
    rows = weights[0].shape[0]
    width = weights[0].shape[1] // (n * groups)
    arrays = list(weights) + ([] if beside is None else [beside])
    total = len(weights) * groups * width + (0 if beside is None else beside.shape[1])

    def kernel(*refs):
        out = refs[-1]
        for i, device in enumerate(devices or range(n)):
            at = 0
            for weight in refs[: len(weights)]:
                for group in range(groups):
                    start = (group * n + device) * width
                    out[i, :, at : at + width] = weight[:, start : start + width]
                    at += width
            if beside is not None:
                out[i, :, at:] = refs[len(weights)][...]

    vmem = pl.BlockSpec(memory_space=pltpu.VMEM)
    return pl.pallas_call(
        kernel,
        out_shape=jax.ShapeDtypeStruct((n, rows, total), bf16),
        in_specs=[vmem] * len(arrays),
        out_specs=vmem,
        compiler_params=pltpu.CompilerParams(vmem_limit_bytes=32 * 1024 * 1024),
    )(*arrays)


def paste_columns(blocks, count, groups, beside=0):
    n, rows, total = blocks.shape
    width = (total - beside) // (count * groups)
    shapes = [jax.ShapeDtypeStruct((rows, groups * n * width), f32)] * count
    if beside:
        shapes.append(jax.ShapeDtypeStruct((rows, n * beside), f32))

    def kernel(ref, *outs):
        for device in range(n):
            at = 0
            for i in range(count):
                for group in range(groups):
                    start = (group * n + device) * width
                    outs[i][:, start : start + width] = ref[device, :, at : at + width].astype(f32)
                    at += width
            if beside:
                start = device * beside
                outs[count][:, start : start + beside] = ref[device, :, at:].astype(f32)

    vmem = pl.BlockSpec(memory_space=pltpu.VMEM)
    return pl.pallas_call(
        kernel,
        out_shape=shapes,
        in_specs=[vmem],
        out_specs=[vmem] * len(shapes),
        compiler_params=pltpu.CompilerParams(vmem_limit_bytes=32 * 1024 * 1024),
    )(blocks)


def ring():
    n = lax.axis_size("ctx")
    return list(range(0, n, 2)) + list(range(n - 1, 0, -2))


def gather_ring(block):
    return lax.all_gather(block, "ctx", axis=0, tiled=True, axis_index_groups=[ring()])


def scatter_ring(total):
    return lax.psum_scatter(
        total, "ctx", scatter_dimension=0, tiled=True, axis_index_groups=[ring()]
    ).astype(f32)


def rearranged(stack, places, columns=False):
    count = len(places)
    rows, width = stack.shape[0] // count, stack.shape[1]

    def kernel(stack_ref, whole, sems):
        copies = []
        for i, to in enumerate(places):
            if columns:
                there = whole.at[:, pl.ds(to * width, width)]
            else:
                there = whole.at[pl.ds(to * rows, rows), :]
            block = stack_ref.at[pl.ds(i * rows, rows), :]
            copies.append(pltpu.make_async_copy(block, there, sems.at[i]))
        for copy in copies:
            copy.start()
        for copy in copies:
            copy.wait()

    shape = (rows, count * width) if columns else stack.shape
    return pl.pallas_call(
        kernel,
        out_shape=jax.ShapeDtypeStruct(shape, stack.dtype),
        in_specs=[pl.BlockSpec(memory_space=pl.ANY)],
        out_specs=pl.BlockSpec(memory_space=pltpu.VMEM),
        scratch_shapes=[pltpu.SemaphoreType.DMA((count,))],
        compiler_params=pltpu.CompilerParams(vmem_limit_bytes=32 * 1024 * 1024),
    )(stack)


def core_swap(block):
    n = lax.axis_size("seq")
    return Box(lax.ppermute(value_of(block), "seq", [(i, i ^ 1) for i in range(n)]))


def gather_seq(x, block):
    far = x.swap(block, 2)
    return [(0, block), (1, core_swap(block)), (2, far), (3, core_swap(far))]


def scatter_seq_near(total, here):
    rows = total.shape[0] // 4

    def piece(offset):
        return lax.dynamic_slice_in_dim(total, (here ^ offset) * rows, rows, 0)

    got = core_swap(jnp.concatenate([piece(3), piece(1)], axis=0).astype(bf16))
    return piece(0) + got.value[rows:].astype(f32), (
        piece(2) + got.value[:rows].astype(f32)
    ).astype(bf16)


def to_owners(part, count, groups, beside=0):
    n = lax.axis_size("ctx")
    blocks = lax.all_to_all(part.reshape(n, -1, part.shape[1]), "ctx", 0, 0, tiled=True)
    return paste_columns(blocks, count, groups, beside)


def tuned(
    hidden_in,
    positions,
    attn_gain,
    w_query,
    w_key,
    w_value,
    w_out,
    mlp_gain,
    w_gate,
    w_up,
    w_down,
    out_grad,
):
    n = lax.axis_size("ctx")
    seqs = lax.axis_size("seq")
    here = lax.axis_index("ctx")
    seq_here = lax.axis_index("seq")
    rows = hidden_in.shape[1]
    weight_rows = w_query.shape[0]
    x = Link("seq", 1)
    place_here = jnp.where(here % 2 == 0, here // 2, n - 1 - here // 2)

    def own_rows(whole):
        return lax.dynamic_slice_in_dim(whole, place_here * rows, rows, 0)

    def from_devices(held):
        return place([part for _, part in held], [seq_here ^ o for o, _ in held])

    own_pos = positions[0].reshape(weight_rows, -1)
    per_row = own_pos.shape[1]
    beside = jnp.concatenate(
        [
            attn_gain[:, None],
            mlp_gain[:, None],
            (own_pos // 64).astype(bf16),
            (own_pos % 64).astype(bf16),
        ],
        axis=1,
    )
    beside = jnp.pad(beside, ((0, 0), (0, 128 - beside.shape[1])))
    x_low = gather_ring(hidden_in[0])
    out_pair = jnp.concatenate([w_out, Link("seq", 1).swap(w_out, 2).value], axis=0)
    down_steps = gather_seq(Link("seq", 1), w_down)
    blocks = cut_columns((w_query, w_key, w_value), 1, beside)
    qkv_mine = lax.all_to_all(blocks, "ctx", 0, 0, tiled=True).reshape(n * weight_rows, -1)
    down_far = down_steps[2][1]
    out_pair, late_gate, late_up, qkv_mine, down_far.value = lax.optimization_barrier(
        (out_pair, w_gate, w_up, qkv_mine, down_far.value)
    )
    qkv_steps = gather_seq(x, qkv_mine)
    out_ring = gather_ring(out_pair)
    blocks = cut_columns((late_gate, late_up), seqs, None)
    gate_up = lax.all_to_all(blocks, "ctx", 0, 0, tiled=True).reshape(n * weight_rows, -1)
    qkv_sub = from_devices(qkv_steps)
    down_sub = from_devices(down_steps)
    pos_cuts = qkv_mine[:, -128:].astype(jnp.int32)
    pos_all = pos_cuts[:, 2 : 2 + per_row] * 64 + pos_cuts[:, 2 + per_row : 2 + 2 * per_row]
    pos_all = pos_all.reshape(n, rows)
    pos_all = jnp.concatenate([pos_all[device] for device in ring()])
    gain1 = qkv_sub[:, -128].astype(f32)
    gain2 = qkv_sub[:, -127].astype(f32)
    qkv_sub = qkv_sub[:, :-128]

    x_all = x_low.astype(f32)
    attn_scale = rms_scale(x_all)
    normed = (x_all * attn_scale * gain1).astype(bf16)
    angles = angle_table(pos_all)
    cosine, sine = jnp.cos(angles), jnp.sin(angles)
    qkv = dot(normed, qkv_sub)
    width = qkv.shape[1] // 3
    query = rotate(qkv[:, :width], cosine, sine).astype(bf16)
    key = rotate(qkv[:, width : 2 * width], cosine, sine).astype(bf16)
    value = qkv[:, 2 * width :].astype(bf16)
    split = width // 2
    halves = [slice(0, split), slice(split, width)]
    att_first, lse_first = attention(*(m[:, halves[0]] for m in (query, key, value)), pos_all)
    value, gate_up = lax.optimization_barrier((value, gate_up))
    att_second, lse_second = attention(*(m[:, halves[1]] for m in (query, key, value)), pos_all)
    att_low = jnp.concatenate([att_first, att_second], axis=1).astype(bf16)
    cut = gate_up.shape[0] // 2
    parts = [gate_up[:cut], gate_up[cut:]]
    far = [x.swap(parts[0], 2)]
    att_low, out_ring, far[0].value = lax.optimization_barrier((att_low, out_ring, far[0].value))
    att_stack = gather_ring(att_low)
    out_other = core_swap(out_ring)
    far.append(x.swap(parts[1], 2))
    full_out = place_pairs(
        [out_ring, out_other.value], [seq_here ^ o for o in (0, 2, 1, 3)], ring()
    )
    late_grad, att_stack = lax.optimization_barrier((out_grad[0], att_stack))
    grad_all = gather_ring(late_grad)
    att_stack, full_out, down_sub = lax.optimization_barrier((att_stack, full_out, down_sub))
    att_low = rearranged(att_stack, ring(), columns=True)

    middle = x_all + dot(att_low, full_out)
    mlp_scale = rms_scale(middle)
    normed_mid = (middle * mlp_scale * gain2).astype(bf16)
    normed_mid, far[1].value = lax.optimization_barrier((normed_mid, far[1].value))
    held = []
    for part, other in zip(parts, far):
        held += [(0, part), (1, core_swap(part)), (2, other), (3, core_swap(other))]
    gate_up = place(
        [part for _, part in held],
        [(seq_here ^ o) * 2 + i // 4 for i, (o, _) in enumerate(held)],
    )
    gate_up_act = dot(normed_mid, gate_up)
    units = gate_up.shape[1] // 2
    gate_act, up_act = gate_up_act[:, :units], gate_up_act[:, units:]
    sig = jax.nn.sigmoid(gate_act)
    inner = (gate_act * sig * up_act).astype(bf16)
    middle_own = own_rows(middle)

    down_part = dot(inner, down_sub).astype(bf16)
    grad_all, down_part = lax.optimization_barrier((grad_all, down_part))
    down_own = scatter_ring(down_part)
    inner_grad = lax.optimization_barrier(dot_cols(grad_all, down_sub))
    gate_grad = (inner_grad * up_act * sig * (1.0 + gate_act * (1.0 - sig))).astype(bf16)
    up_grad = (inner_grad * gate_act * sig).astype(bf16)
    gate_up_grad = lax.optimization_barrier(jnp.concatenate([gate_grad, up_grad], axis=1))
    mid_grad_part = dot_cols(gate_up_grad, gate_up).astype(bf16)
    gate_up_near, gate_up_far = scatter_seq_near(dot_rows(normed_mid, gate_up_grad), seq_here)
    mid_grad_in = scatter_ring(mid_grad_part)
    down_weight_part = dot_rows(inner, grad_all)
    gate_up_far = x.swap(gate_up_far, 2)
    mid_grad_in, down_weight_part, down_own, gate_up_far.value = lax.optimization_barrier(
        (mid_grad_in, down_weight_part, down_own, gate_up_far.value)
    )

    mid_scale = own_rows(mlp_scale)
    mid_unit = middle_own * mid_scale
    mid_term = mid_grad_in * gain2
    middle_grad = out_grad[0].astype(f32) + mid_scale * (
        mid_term - mid_unit * jnp.mean(mid_unit * mid_term, axis=-1, keepdims=True)
    )
    mlp_gain_part = jnp.sum(mid_grad_in * mid_unit, axis=0)
    middle_low = middle_grad.astype(bf16)
    att_grad = dot_cols(middle_low, full_out).astype(bf16)
    blocks = cut_columns((att_grad,), 1, None, ring())
    att_grad = lax.all_to_all(blocks, "ctx", 0, 0, tiled=True, axis_index_groups=[ring()])
    att_grad = att_grad.reshape(n * rows, -1)
    middle_low_all = gather_ring(middle_low)

    gate_up_sum = (gate_up_near + gate_up_far.value.astype(f32)).astype(bf16)
    att_grad, gate_up_sum = lax.optimization_barrier((att_grad, gate_up_sum))
    gate_sum, up_sum = (
        lax.all_to_all(part.reshape(n, weight_rows, -1), "ctx", 0, 0, tiled=True)
        for part in (gate_up_sum[:, :units], gate_up_sum[:, units:])
    )
    grads = [
        attention_back(
            *(m[:, halves[0]] for m in (query, key, value)), pos_all, att_first, lse_first, att_grad[:, halves[0]]
        )
    ]
    down_weight_near, down_weight_far = scatter_seq_near(down_weight_part, seq_here)
    att_grad, down_weight_far, grads[0] = lax.optimization_barrier(
        (att_grad, down_weight_far, grads[0])
    )
    down_weight_far = x.swap(down_weight_far, 2)
    grads.append(
        attention_back(
            *(m[:, halves[1]] for m in (query, key, value)), pos_all, att_second, lse_second, att_grad[:, halves[1]]
        )
    )
    query_acc, key_acc, value_acc = (jnp.concatenate(pair, axis=1) for pair in zip(*grads))
    qkv_grad = jnp.concatenate(
        [rotate(query_acc, cosine, -sine), rotate(key_acc, cosine, -sine), value_acc], axis=1
    ).astype(bf16)
    out_rows = w_out.shape[0]
    att_sub = jnp.concatenate(
        [
            lax.dynamic_slice_in_dim(att_low, (i * n + here) * out_rows, out_rows, 1)
            for i in range(seqs)
        ],
        axis=1,
    )
    w_out_near, w_out_far = scatter_seq_near(dot_rows(att_sub, middle_low_all), seq_here)
    hidden_out = (middle_own + down_own).astype(bf16)
    qkv_grad, gate_sum = lax.optimization_barrier((qkv_grad, gate_sum))
    normed_grad_part = dot_cols(qkv_grad, qkv_sub)
    attn_gain_part = jnp.sum(normed_grad_part * (x_all * attn_scale), axis=0)
    beside = jnp.stack([attn_gain_part, mlp_gain_part], axis=1)
    beside = jnp.pad(beside, ((0, 0), (0, 126)))
    qkv_part = jnp.concatenate([dot_rows(normed, qkv_grad), beside], axis=1)
    qkv_near, qkv_far = scatter_seq_near(qkv_part, seq_here)
    normed_grad = scatter_ring(normed_grad_part.astype(bf16))
    qkv_far = Link("seq", 1).swap(qkv_far, 2)
    qkv_far.value, up_sum, w_out_far = lax.optimization_barrier((qkv_far.value, up_sum, w_out_far))
    qkv_sum = (qkv_near + qkv_far.value.astype(f32)).astype(bf16)
    w_query_grad, w_key_grad, w_value_grad, gain_grads = to_owners(qkv_sum, 3, 1, 128)
    gain_grads = gain_grads.astype(f32).reshape(weight_rows, n, 128).sum(axis=1)
    w_out_grad = w_out_near + Link("seq", 1).swap(w_out_far, 2).value.astype(f32)
    w_down_grad = down_weight_near + down_weight_far.value.astype(f32)
    w_out_grad, w_down_grad, normed_grad = lax.optimization_barrier(
        (w_out_grad, w_down_grad, normed_grad)
    )
    (w_gate_grad,) = paste_columns(gate_sum, 1, seqs)
    (w_up_grad,) = paste_columns(up_sum, 1, seqs)

    own_scale = own_rows(attn_scale)
    own_unit = hidden_in[0].astype(f32) * own_scale
    attn_term = normed_grad * gain1
    hidden_grad = middle_grad + own_scale * (
        attn_term - own_unit * jnp.mean(own_unit * attn_term, axis=-1, keepdims=True)
    )
    return (
        hidden_out[None],
        hidden_grad[None],
        gain_grads[:, 0],
        w_query_grad,
        w_key_grad,
        w_value_grad,
        w_out_grad,
        gain_grads[:, 1],
        w_gate_grad,
        w_up_grad,
        w_down_grad,
    )


def solution(mesh):
    tokens = P("seq", "ctx", None)
    whole = P(("seq", "ctx"), None)
    gain = P(("seq", "ctx"))
    local = tuned if mesh.shape["ctx"] == 8 and mesh.shape["seq"] == 4 else plain
    return jax.shard_map(
        local,
        mesh=mesh,
        in_specs=(
            tokens,
            P("seq", "ctx"),
            gain,
            whole,
            whole,
            whole,
            whole,
            gain,
            whole,
            whole,
            whole,
            tokens,
        ),
        out_specs=(tokens, tokens, gain, whole, whole, whole, whole, gain, whole, whole, whole),
        check_vma=False,
    )
```
